128 devices in a mesh: rep: 32 (over y, x, z_lo), grp: 4 (over z_hi, core).
Axes of the slice: x: 4, y: 4, z: 4 (z_hi: 2, z_lo: 2; z = z_hi * 2 + z_lo), core: 2. Of those that a mesh axis runs over, the one named last changes fastest.
Arguments:
- block_input: bfloat16 [32, 1024, 1088], P('rep', 'grp'), may hold values from -6 to 6
- segment_ids: int32 [32, 1024], P('rep'), may hold values from 0 to 2, as said below
- attn_gain: bfloat16 [1088], P('grp'), may hold values from 0.5 to 1.5
- attn_shift: bfloat16 [1088], P('grp'), may hold values from -1.75 to 1.75
- w_qkv: bfloat16 [1088, 3264], P('grp'), may hold values from -0.1875 to 0.1875
- bias_query: bfloat16 [1088], P('grp'), may hold values from -1.75 to 1.75
- bias_value: bfloat16 [1088], P('grp'), may hold values from -1.75 to 1.75
- w_out: bfloat16 [1088, 1088], P('grp'), may hold values from -0.5 to 0.5
- bias_out: bfloat16 [1088], P('grp'), may hold values from -1.75 to 1.75
- mlp_gain: bfloat16 [1088], P('grp'), may hold values from 0.5 to 1.5
- mlp_shift: bfloat16 [1088], P('grp'), may hold values from -1.75 to 1.75
- w_up: bfloat16 [1088, 4352], P('grp'), may hold values from -0.1875 to 0.1875
- bias_up: bfloat16 [4352], P('grp'), may hold values from -1.75 to 1.75
- w_down: bfloat16 [4352, 1088], P('grp'), may hold values from -0.09375 to 0.09375
- bias_down: bfloat16 [1088], P('grp'), may hold values from -1.75 to 1.75
- cotangent: bfloat16 [32, 1024, 1088], P('rep', 'grp'), may hold values from -6 to 6
Outputs:
- block_output: float32 [32, 1024, 1088], P('rep', 'grp')
- grad_input: float32 [32, 1024, 1088], P('rep', 'grp')
- grad_attn_gain: float32 [1088], P('grp')
- grad_attn_shift: float32 [1088], P('grp')
- grad_w_qkv: float32 [1088, 3264], P('grp')
- grad_bias_query: float32 [1088], P('grp')
- grad_bias_value: float32 [1088], P('grp')
- grad_w_out: float32 [1088, 1088], P('grp')
- grad_bias_out: float32 [1088], P('grp')
- grad_mlp_gain: float32 [1088], P('grp')
- grad_mlp_shift: float32 [1088], P('grp')
- grad_w_up: float32 [1088, 4352], P('grp')
- grad_bias_up: float32 [4352], P('grp')
- grad_w_down: float32 [4352, 1088], P('grp')
- grad_bias_down: float32 [1088], P('grp')
The draws below stay inside these ranges and needn't reach their ends.
Inputs may be any that keep to these rules, and one draw needn't show every extreme that they name: `segment_ids`: in each row the first document holds fewer than 128 tokens, the second runs until fewer than 128 tokens remain, and the third holds the rest; numbers never fall along a row.
All inputs are finite; a program needn't handle non-finite values.
Results may differ from the reference program's by a relative error of at most 0.015.
Values may be sent and summed in bfloat16 or wider, within the bound.
No kernel may reach another device: no remote copies, remote signals or barrier semaphores. Data moves between devices by JAX's collectives and lax.ppermute only.
A program may use at most 192 MiB of HBM per device.

```python
from functools import partial
import jax
import jax.numpy as jnp
from jax import lax

D = 1088
HEADS = 17
HEAD = 64
FF = 4352
TOK_DEV = 256
SEQ = 1024
SEQS = 32


def draw_segment_ids(key, part):
    key = jax.random.fold_in(key, 7)
    key_head, key_tail = jax.random.split(key)
    head = jax.random.randint(key_head, (SEQS,), 1, TOK_DEV // 2)
    tail = jax.random.randint(key_tail, (SEQS,), 1, TOK_DEV // 2)
    places = jnp.arange(SEQ)
    first = (places[None, :] >= head[:, None]).astype(jnp.int32)
    second = (places[None, :] >= (SEQ - tail)[:, None]).astype(jnp.int32)
    return first + second


def steps_of(key, dims, pieces, least, high):
    level = 1.0
    for position, parts in pieces:
        steps = jax.random.uniform(jax.random.fold_in(jax.random.fold_in(key, 6), position), (parts,), jnp.float32, least / len(pieces), high / len(pieces))
        level = level * jnp.repeat(jnp.exp(steps), dims[position] // parts).reshape((-1,) + (1,) * (len(dims) - 1 - position))
    return level


def scatter_about(key, dims, width, bound, cuts=(), dtype=jnp.bfloat16):
    result = jax.random.normal(key, dims, jnp.float32) * width
    if len(cuts) > 0:
        result = steps_of(key, dims, cuts, -0.22, 0.18) * result
    return jnp.clip(result, min=-bound, max=bound).astype(dtype)


def setup_inputs(seed: int = 0) -> dict:
    splits = jax.random.split(jax.random.key(seed), 17)
    return {
        "block_input": scatter_about(splits[0], (SEQS, SEQ, D), 1.0, 6.0, ((0, 32), (1, 4))),
        "segment_ids": draw_segment_ids(jax.random.fold_in(splits[16], 71), 0),
        "attn_gain": jnp.clip(1.0 + 0.1 * jax.random.normal(splits[2], (D,), jnp.float32), 0.5, 1.5).astype(jnp.bfloat16),
        "attn_shift": scatter_about(splits[3], (D,), 0.3, 1.75, ((0, 4),)),
        "w_qkv": scatter_about(splits[4], (D, 3 * D), D ** -0.5, 0.1875, ((0, 4),)),
        "bias_query": scatter_about(splits[5], (D,), 0.3, 1.75, ((0, 4),)),
        "bias_value": scatter_about(splits[6], (D,), 0.3, 1.75, ((0, 4),)),
        "w_out": scatter_about(splits[7], (D, D), (D // 8) ** -0.5, 0.5, ((0, 4),)),
        "bias_out": scatter_about(splits[8], (D,), 0.3, 1.75, ((0, 4),)),
        "mlp_gain": jnp.clip(1.0 + 0.1 * jax.random.normal(splits[9], (D,), jnp.float32), 0.5, 1.5).astype(jnp.bfloat16),
        "mlp_shift": scatter_about(splits[10], (D,), 0.3, 1.75, ((0, 4),)),
        "w_up": scatter_about(splits[11], (D, FF), D ** -0.5, 0.1875, ((0, 4),)),
        "bias_up": scatter_about(splits[12], (FF,), 0.3, 1.75, ((0, 4),)),
        "w_down": scatter_about(splits[13], (FF, D), FF ** -0.5, 0.09375, ((0, 4),)),
        "bias_down": scatter_about(splits[14], (D,), 0.3, 1.75, ((0, 4),)),
        "cotangent": scatter_about(splits[15], (SEQS, SEQ, D), 1.0, 6.0, ((0, 32), (1, 4))),
    }


@jax.custom_vjp
def low(v):
    return lax.optimization_barrier(v.astype(jnp.bfloat16)).astype(jnp.float32)

@jax.custom_vjp
def low_back(v):
    return v

def low_keep(v):
    return (low(v), None)

def low_pass(kept, grad):
    return (grad,)

def back_keep(v):
    return (v, None)

def back_low(kept, grad):
    return (low(grad),)
low.defvjp(low_keep, low_pass)
low_back.defvjp(back_keep, back_low)

def matmul(left, right):
    return jnp.dot(left, right, precision=lax.Precision.HIGHEST, preferred_element_type=jnp.float32)

def layer_norm(values, gain, shift):
    centre = values - lax.optimization_barrier(jnp.mean(values, axis=-1, keepdims=True))
    spread = lax.optimization_barrier(jnp.mean(centre * centre, axis=-1, keepdims=True))
    return centre * lax.rsqrt(spread + 1e-05) * gain + shift

def forward(segments, hidden_in, attn_gain, attn_shift, w_qkv, bias_query, bias_value, w_out, bias_out, mlp_gain, mlp_shift, w_up, bias_up, w_down, bias_down):
    length = hidden_in.shape[0]
    normed = low(layer_norm(hidden_in, attn_gain, attn_shift))
    project = matmul(normed, w_qkv)
    queries = low(low_back(project[:, :D] + bias_query))
    keys_all = low(low_back(project[:, D:2 * D]))
    values_all = low(low_back(project[:, 2 * D:] + bias_value))
    heads_query = queries.reshape(length, HEADS, HEAD)
    heads_key = keys_all.reshape(length, HEADS, HEAD)
    heads_value = values_all.reshape(length, HEADS, HEAD)
    raw = jnp.einsum('qhd,khd->hqk', heads_query, heads_key, precision=lax.Precision.HIGHEST)
    scores = low_back(raw * 0.125)
    places = jnp.arange(length)
    allowed = (segments[:, None] == segments[None, :]) & (places[:, None] >= places[None, :])
    scores = jnp.where(allowed[None], scores, -1e+30)
    probs = low(jax.nn.softmax(scores, axis=-1))
    mixed = jnp.einsum('hqk,khd->qhd', probs, heads_value, precision=lax.Precision.HIGHEST).reshape(length, D)
    mixed = low(low_back(mixed))
    attended = low_back(matmul(mixed, w_out) + bias_out)
    middle = hidden_in + attended
    normed_two = low(layer_norm(middle, mlp_gain, mlp_shift))
    upper = low_back(matmul(normed_two, w_up) + bias_up)
    activated = low(jax.nn.gelu(upper, approximate=False))
    branch = low_back(matmul(activated, w_down) + bias_down)
    return middle + branch

def reference(block_input, segment_ids, attn_gain, attn_shift, w_qkv, bias_query, bias_value, w_out, bias_out, mlp_gain, mlp_shift, w_up, bias_up, w_down, bias_down, cotangent):
    params = tuple((piece.astype(jnp.float32) for piece in (attn_gain, attn_shift, w_qkv, bias_query, bias_value, w_out, bias_out, mlp_gain, mlp_shift, w_up, bias_up, w_down, bias_down)))

    def one_sequence(totals, item):
        hidden_in, segments, upstream = item
        output, backward = jax.vjp(partial(forward, segments), hidden_in.astype(jnp.float32), *params)
        grads = backward(upstream.astype(jnp.float32))
        totals = tuple((total + grad for total, grad in zip(totals, grads[1:])))
        return (totals, (output, grads[0]))
    start = tuple((jnp.zeros(piece.shape, jnp.float32) for piece in params))
    totals, (outputs, grad_inputs) = lax.scan(one_sequence, start, (block_input, segment_ids, cotangent))
    return (outputs, grad_inputs, totals[0], totals[1], totals[2], totals[3], totals[4], totals[5], totals[6], totals[7], totals[8], totals[9], totals[10], totals[11], totals[12])
```

```python
import jax
import jax.numpy as jnp
from jax import lax
from jax.experimental import pallas as pl
from jax.experimental.pallas import tpu as pltpu
from jax.sharding import Mesh
from jax.sharding import PartitionSpec as P

D = 1088
HEADS = 17
HEAD = 64
QUART = 272
SLICE = 68
PAD = 72
VECTOR = 204
AXES = ("y", "x", "zl", "zh", "c")
BF = jnp.bfloat16
F32 = jnp.float32


def layer_norm(values, gain, shift):
    centre = values - jnp.mean(values, axis=-1, keepdims=True)
    spread = jnp.mean(centre * centre, axis=-1, keepdims=True)
    return centre * lax.rsqrt(spread + 1e-05) * gain + shift


def exact_gelu(values):
    return jax.nn.gelu(values, approximate=False)


def masked_scores(heads_query, heads_key, allowed):
    raw = (
        jnp.einsum("qhd,khd->hqk", heads_query, heads_key, preferred_element_type=F32) * 0.125
    )
    return jnp.where(allowed[None], raw, -1e30)


def transpose_dot(left, right):
    return lax.dot_general(left, right, (((0,), (0,)), ((), ())), preferred_element_type=F32)


def swap_core(x):
    return lax.ppermute(x, "c", [(0, 1), (1, 0)])


def swap_half(x):
    return lax.ppermute(x, "zh", [(0, 1), (1, 0)])


def swap_near(x):
    return lax.ppermute(x, "zl", [(0, 1), (1, 0)])


def swap_far(x):
    return lax.ppermute(x, ("zl", "zh"), [(0, 3), (3, 0), (1, 2), (2, 1)])


def depth_sum(values, zh):
    mine = jnp.where(zh == 0, values[0], values[1]).astype(F32)
    other = jnp.where(zh == 0, values[1], values[0])
    near = (mine + swap_far(other).astype(F32)).astype(BF)
    return (near.astype(F32) + swap_near(near).astype(F32)).astype(BF)


def assemble_kernel(*refs):
    *parts, out, sems = refs
    rows = out.shape[0] // 4
    rank = lax.axis_index("zh") * 2 + lax.axis_index("c")
    copies = []
    start, flip = 0, 0
    for ref in parts:
        size = min(ref.shape[0], rows - start)
        at = jnp.bitwise_xor(rank, flip) * rows + start
        copy = pltpu.make_async_copy(
            ref.at[pl.ds(0, size)],
            out.at[pl.ds(pl.multiple_of(at, 16), size)],
            sems.at[len(copies)],
        )
        copy.start()
        copies.append(copy)
        start += size
        if start == rows:
            start, flip = 0, flip + 1
    for copy in copies:
        copy.wait()


def assemble(rows, *parts):
    columns = parts[0].shape[1]
    return pl.pallas_call(
        assemble_kernel,
        out_shape=jax.ShapeDtypeStruct((rows * 4, columns), BF),
        in_specs=[pl.BlockSpec(memory_space=pltpu.VMEM)] * len(parts),
        out_specs=pl.BlockSpec(memory_space=pl.ANY),
        scratch_shapes=[pltpu.SemaphoreType.DMA((len(parts),))],
        compiler_params=pltpu.CompilerParams(vmem_limit_bytes=24 * 2**20),
        cost_estimate=pl.CostEstimate(
            flops=0, bytes_accessed=rows * columns * 16, transcendentals=0
        ),
    )(*parts)


def gather_direct(shard):
    far = swap_far(shard)
    return shard, swap_core(shard), far, swap_core(far)


def gather_spread(shard, spot):
    unit = shard.shape[0] // 17
    main = shard[: 16 * unit].reshape(16, unit, shard.shape[1])
    tail = shard[16 * unit :]
    piece = lax.dynamic_index_in_dim(main, spot, 0, keepdims=False)
    got = swap_far(jnp.concatenate([piece, tail]))
    far = lax.all_gather(got[:unit], ("y", "x"), axis=0, tiled=True)
    rest = got[unit:]
    return assemble(
        shard.shape[0], shard, swap_core(shard), far, rest, swap_core(far), swap_core(rest)
    )


def body(
    block_input,
    segment_ids,
    attn_gain,
    attn_shift,
    w_qkv,
    bias_query,
    bias_value,
    w_out,
    bias_out,
    mlp_gain,
    mlp_shift,
    w_up,
    bias_up,
    w_down,
    bias_down,
    cotangent,
):
    core, zh = lax.axis_index("c"), lax.axis_index("zh")
    rank = zh * 2 + core
    spot = lax.axis_index("y") * 4 + lax.axis_index("x")
    small = jnp.concatenate(
        [
            attn_gain,
            attn_shift,
            bias_query,
            bias_value,
            bias_out,
            mlp_gain,
            mlp_shift,
            bias_up,
            bias_down,
        ]
    )
    small = jnp.pad(small[None], ((0, 15), (0, 0)))
    qkv_parts = gather_direct(jnp.concatenate([w_qkv, small]))
    smalls = [value[QUART].astype(F32) for value in qkv_parts]
    full_qkv = assemble(QUART, *qkv_parts)
    full_out = assemble(QUART, *gather_direct(w_out))
    full_up = gather_spread(w_up, spot)
    full_down = gather_spread(w_down, spot)

    ordered = []
    for index in range(4):
        value = smalls[index]
        for at in range(1, 4):
            value = jnp.where(rank == at, smalls[index ^ at], value)
        ordered.append(value)
    ordered = jnp.stack(ordered)

    def vector(start, size):
        return ordered[:, start : start + size].reshape(-1)

    gain_one, shift_one, query_bias, value_bias, out_bias, gain_two, shift_two = (
        vector(QUART * index, QUART) for index in range(7)
    )
    up_bias = vector(7 * QUART, D)
    down_bias = vector(11 * QUART, QUART)

    rows = block_input.shape[1]
    hidden_in = block_input[0].astype(F32)
    segments = segment_ids[0]
    upstream = cotangent[0]

    normed = layer_norm(hidden_in, gain_one, shift_one).astype(BF)
    project = jnp.dot(normed, full_qkv, preferred_element_type=F32)
    queries = (project[:, :D] + query_bias).astype(BF)
    both_mine = jnp.concatenate(
        [project[:, D : 2 * D].astype(BF), (project[:, 2 * D :] + value_bias).astype(BF)], axis=1
    )
    both_half = swap_half(both_mine)
    both_all = jnp.concatenate(
        [both_mine, swap_core(both_mine), both_half, swap_core(both_half)]
    )
    length = both_all.shape[0]
    heads_query = queries.reshape(rows, HEADS, HEAD)
    heads_key = both_all[:, :D].reshape(length, HEADS, HEAD)
    heads_value = both_all[:, D:].reshape(length, HEADS, HEAD)
    query_places = rank * rows + jnp.arange(rows)
    key_places = jnp.concatenate(
        [jnp.bitwise_xor(rank, flip) * rows + jnp.arange(rows) for flip in range(4)]
    )
    key_segments = jnp.concatenate(
        [
            lax.dynamic_slice_in_dim(segments, jnp.bitwise_xor(rank, flip) * rows, rows)
            for flip in range(4)
        ]
    )
    query_segments = key_segments[:rows]
    allowed = (query_segments[:, None] == key_segments[None, :]) & (
        query_places[:, None] >= key_places[None, :]
    )
    scores = masked_scores(heads_query, heads_key, allowed)
    highest = jnp.max(scores, axis=-1, keepdims=True)
    log_total = highest + jnp.log(jnp.sum(jnp.exp(scores - highest), axis=-1, keepdims=True))
    probs_low = jnp.exp(scores - log_total).astype(BF)
    mixed = jnp.einsum("hqk,khd->qhd", probs_low, heads_value, preferred_element_type=F32)
    mixed = mixed.reshape(rows, D).astype(BF)
    middle = hidden_in + jnp.dot(mixed, full_out, preferred_element_type=F32) + out_bias
    normed_two = layer_norm(middle, gain_two, shift_two).astype(BF)
    upper = jnp.dot(normed_two, full_up, preferred_element_type=F32) + up_bias
    activated = exact_gelu(upper).astype(BF)
    block_output = middle + jnp.dot(activated, full_down, preferred_element_type=F32) + down_bias

    def paired(value):
        return jnp.concatenate([value, swap_core(value)])

    def paired_columns(value, pad=False):
        width = value.shape[1] // 4
        blocks = [value[:, at * width : (at + 1) * width] for at in range(4)]

        def joined(one, two):
            if not pad:
                return jnp.concatenate([one, two], axis=1)
            empty = jnp.zeros((rows, PAD - SLICE), BF)
            parts = []
            for block in (one, two):
                for at in range(4):
                    parts += [block[:, at * SLICE : (at + 1) * SLICE], empty]
            return jnp.concatenate(parts, axis=1)

        even, odd = joined(blocks[0], blocks[2]), joined(blocks[1], blocks[3])
        mine = jnp.where(core == 0, even, odd)
        other = jnp.where(core == 0, odd, even)
        return jnp.concatenate([mine, swap_core(other)])

    def weight_grad(left, right, pieces):
        product = transpose_dot(left, right).astype(BF)
        return product.reshape(2, pieces, -1, D).transpose(1, 0, 2, 3)

    def across(value):
        rest = value.shape[2]
        value = lax.psum_scatter(
            value.reshape(32 * rest, D), ("y", "x"), scatter_dimension=0, tiled=True
        )
        return value.reshape(2, rest, D)

    upstream_wide = upstream.astype(F32)
    upstream_pair = paired(upstream)
    grad_down_bias = jnp.sum(upstream_wide, axis=0)
    grad_down = weight_grad(paired_columns(activated), upstream_pair, 8)

    d_activated = jnp.dot(upstream, full_down.T, preferred_element_type=F32)
    gelu_back = jax.vjp(exact_gelu, upper)[1]
    d_upper = gelu_back(d_activated)[0].astype(BF)
    grad_up_bias = jnp.sum(d_upper.astype(F32), axis=0)
    normed_two_pair, d_upper_pair = paired_columns(normed_two), paired(d_upper)
    grad_up = [
        weight_grad(normed_two_pair, d_upper_pair[:, at * D : (at + 1) * D], 2) for at in range(4)
    ]
    mlp_part = across(jnp.concatenate(grad_up + [grad_down]))

    d_normed_two = jnp.dot(d_upper, full_up.T, preferred_element_type=F32)
    norm_two_back = jax.vjp(layer_norm, middle, gain_two, shift_two)[1]
    d_middle_part, grad_gain_two, grad_shift_two = norm_two_back(d_normed_two)
    d_middle = upstream_wide + d_middle_part
    d_attended = d_middle.astype(BF)
    grad_out_bias = jnp.sum(d_attended.astype(F32), axis=0)
    grad_out = weight_grad(paired_columns(mixed, True), paired(d_attended), 4)

    d_mixed = jnp.dot(d_attended, full_out.T, preferred_element_type=F32).astype(BF)
    heads_d_mixed = d_mixed.reshape(rows, HEADS, HEAD)
    scores = masked_scores(heads_query, heads_key, allowed)
    probs = jnp.exp(scores - log_total)
    d_probs = jnp.einsum("qhd,khd->hqk", heads_d_mixed, heads_value, preferred_element_type=F32)
    centred = jnp.sum(probs * d_probs, axis=-1, keepdims=True)
    d_scores = (probs * (d_probs - centred)).astype(BF)
    d_queries = (
        jnp.einsum("hqk,khd->qhd", d_scores, heads_key, preferred_element_type=F32) * 0.125
    )
    d_keys_part = (
        jnp.einsum("hqk,qhd->khd", d_scores, heads_query, preferred_element_type=F32) * 0.125
    )
    d_values_part = jnp.einsum(
        "hqk,qhd->khd", probs.astype(BF), heads_d_mixed, preferred_element_type=F32
    )
    d_both = jnp.concatenate(
        [d_keys_part.astype(BF).reshape(length, D), d_values_part.astype(BF).reshape(length, D)],
        axis=1,
    ).reshape(4, rows, 2 * D)
    beside = swap_core(d_both[1::2])
    d_half = swap_half((d_both[2].astype(F32) + beside[1].astype(F32)).astype(BF))
    d_both_low = (
        d_both[0].astype(F32) + beside[0].astype(F32) + d_half.astype(F32)
    ).astype(BF)
    d_queries_low = d_queries.reshape(rows, D).astype(BF)
    d_project = jnp.concatenate([d_queries_low, d_both_low], axis=1)
    grad_query_bias = jnp.sum(d_queries_low.astype(F32), axis=0)
    grad_value_bias = jnp.sum(d_both_low[:, D:].astype(F32), axis=0)
    normed_pair, d_project_pair = paired_columns(normed, True), paired(d_project)
    grad_qkv = [
        weight_grad(normed_pair, d_project_pair[:, at * D : (at + 1) * D], 4) for at in range(3)
    ]
    d_normed = jnp.dot(d_project, full_qkv.T, preferred_element_type=F32)
    norm_one_back = jax.vjp(layer_norm, hidden_in, gain_one, shift_one)[1]
    d_input_part, grad_gain_one, grad_shift_one = norm_one_back(d_normed)
    grad_input = d_middle + d_input_part

    vectors = jnp.concatenate(
        [
            value.reshape(4, -1)
            for value in (
                grad_gain_one,
                grad_shift_one,
                grad_query_bias,
                grad_value_bias,
                grad_out_bias,
                grad_gain_two,
                grad_shift_two,
                grad_down_bias,
                grad_up_bias,
            )
        ],
        axis=1,
    )
    even, odd = vectors[0::2], vectors[1::2]
    mine = jnp.where(core == 0, even, odd)
    other = jnp.where(core == 0, odd, even)
    mine = (mine + swap_core(other.astype(BF)).astype(F32)).astype(BF)
    mine = mine.reshape(2, 16, VECTOR).transpose(1, 0, 2)[:, :, None]

    grad_attn = jnp.concatenate(grad_qkv + [grad_out])
    grad_attn = lax.dynamic_update_slice(grad_attn, mine, (0, 0, SLICE, 0))
    mlp_part, grad_attn = lax.optimization_barrier((mlp_part, grad_attn))
    mlp_part = depth_sum(mlp_part, zh)
    attn_part = depth_sum(lax.optimization_barrier(across(grad_attn)), zh)

    mlp = lax.all_gather(mlp_part, ("y", "x"), axis=0, tiled=True)
    grad_up = jnp.concatenate(
        [mlp[at * QUART : (at + 1) * QUART].astype(F32) for at in range(4)], axis=1
    )
    grad_down = mlp[D:].astype(F32)
    attn = lax.all_gather(attn_part, ("y", "x"), axis=0, tiled=True).reshape(16, PAD, D)
    vectors = attn[:, SLICE, :VECTOR].reshape(-1).astype(F32)
    attn = attn[:, :SLICE].astype(F32).reshape(4, QUART, D)
    grad_qkv = jnp.concatenate([attn[0], attn[1], attn[2]], axis=1)
    grad_out = attn[3]

    def owned(start, size):
        return vectors[start : start + size]

    return (
        block_output[None],
        grad_input[None],
        owned(0, QUART),
        owned(QUART, QUART),
        grad_qkv,
        owned(2 * QUART, QUART),
        owned(3 * QUART, QUART),
        grad_out,
        owned(4 * QUART, QUART),
        owned(5 * QUART, QUART),
        owned(6 * QUART, QUART),
        grad_up,
        owned(8 * QUART, D),
        grad_down,
        owned(7 * QUART, QUART),
    )


def solution(mesh):
    grid = Mesh(mesh.devices.reshape(4, 4, 2, 2, 2), AXES)
    rep, grp = ("y", "x", "zl"), ("zh", "c")
    tokens = P(rep, grp, None)
    vector, matrix = P(grp), P(grp, None)
    params = (
        vector,
        vector,
        matrix,
        vector,
        vector,
        matrix,
        vector,
        vector,
        vector,
        matrix,
        vector,
        matrix,
        vector,
    )
    return jax.shard_map(
        body,
        mesh=grid,
        in_specs=(tokens, P(rep, None)) + params + (tokens,),
        out_specs=(tokens, tokens) + params,
        check_vma=False,
    )
```

```python
import functools

import jax
import jax.numpy as jnp
from jax import lax
from jax.experimental import pallas as pl
from jax.experimental.pallas import tpu as pltpu
from jax.sharding import Mesh
from jax.sharding import PartitionSpec as P

D = 1088
HEADS = 17
HEAD = 64
QUART = 272
SLICE = 68
PAD = 72
VECTOR = 204
AXES = ("y", "x", "zl", "zh", "c")
BF = jnp.bfloat16
F32 = jnp.float32


def layer_norm(values, gain, shift):
    centre = values - jnp.mean(values, axis=-1, keepdims=True)
    spread = jnp.mean(centre * centre, axis=-1, keepdims=True)
    return centre * lax.rsqrt(spread + 1e-05) * gain + shift


def exact_gelu(values):
    return jax.nn.gelu(values, approximate=False)


def swap_core(x):
    return lax.ppermute(x, "c", [(0, 1), (1, 0)])


def swap_half(x):
    return lax.ppermute(x, "zh", [(0, 1), (1, 0)])


def swap_near(x):
    return lax.ppermute(x, "zl", [(0, 1), (1, 0)])


def swap_far(x):
    return lax.ppermute(x, ("zl", "zh"), [(0, 3), (3, 0), (1, 2), (2, 1)])


def depth_sum(values, zh):
    mine = jnp.where(zh == 0, values[0], values[1]).astype(F32)
    other = jnp.where(zh == 0, values[1], values[0])
    near = (mine + swap_far(other).astype(F32)).astype(BF)
    return (near.astype(F32) + swap_near(near).astype(F32)).astype(BF)


def assemble_kernel(spots, *refs):
    *parts, out, sems = refs
    rows = out.shape[0] // 4
    rank = lax.axis_index("zh") * 2 + lax.axis_index("c")
    quarter = lax.axis_index("y") % 2 * 2 + lax.axis_index("x") % 2
    copies = []
    for ref, (flip, start, turn, size) in zip(parts, spots):
        at = jnp.bitwise_xor(rank, flip) * rows + start
        if turn is not None:
            at = at + jnp.bitwise_xor(quarter, turn) * size
        copy = pltpu.make_async_copy(
            ref.at[pl.ds(0, size)],
            out.at[pl.ds(pl.multiple_of(at, 16), size)],
            sems.at[len(copies)],
        )
        copy.start()
        copies.append(copy)
    for copy in copies:
        copy.wait()


def assemble(rows, parts, spots):
    columns = parts[0].shape[1]
    return pl.pallas_call(
        functools.partial(assemble_kernel, spots),
        out_shape=jax.ShapeDtypeStruct((rows * 4, columns), BF),
        in_specs=[pl.BlockSpec(memory_space=pltpu.VMEM)] * len(parts),
        out_specs=pl.BlockSpec(memory_space=pl.ANY),
        scratch_shapes=[pltpu.SemaphoreType.DMA((len(parts),))],
        compiler_params=pltpu.CompilerParams(vmem_limit_bytes=24 * 2**20),
        cost_estimate=pl.CostEstimate(
            flops=0, bytes_accessed=rows * columns * 16, transcendentals=0
        ),
    )(*parts)


def dot_nt(left, right):
    return lax.dot_general(left, right, (((1,), (1,)), ((), ())), preferred_element_type=F32)


def dot_tn(left, right):
    return lax.dot_general(left, right, (((0,), (0,)), ((), ())), preferred_element_type=F32)


def attend_forward_kernel(q_ref, k_ref, v_ref, mask_ref, mixed_ref, total_ref):
    mask = mask_ref[...]
    queries, keys, values = q_ref[...], k_ref[...], v_ref[...]
    mixed, totals = [], []
    for head in range(2):
        lanes = slice(head * HEAD, (head + 1) * HEAD)
        scores = dot_nt(queries[:, lanes], keys[:, lanes]) * 0.125 + mask
        highest = jnp.max(scores, axis=1, keepdims=True)
        powers = jnp.exp(scores - highest)
        total = jnp.sum(powers, axis=1, keepdims=True)
        probs = (powers * (1.0 / total)).astype(BF)
        value = jnp.dot(probs, values[:, lanes], preferred_element_type=F32)
        mixed.append(value)
        totals.append(jnp.broadcast_to(highest + jnp.log(total), value.shape))
    mixed_ref[...] = jnp.concatenate(mixed, axis=1).astype(BF)
    total_ref[...] = jnp.concatenate(totals, axis=1)


def attend_backward_kernel(
    q_ref, k_ref, v_ref, mask_ref, total_ref, d_mixed_ref, dq_ref, keep_ref, send_ref
):
    mask = mask_ref[...]
    queries, keys, values = q_ref[...], k_ref[...], v_ref[...]
    totals, d_mixed = total_ref[...], d_mixed_ref[...]
    d_query, d_key, d_value = [], [], []
    for head in range(2):
        lanes = slice(head * HEAD, (head + 1) * HEAD)
        query, key, upstream = queries[:, lanes], keys[:, lanes], d_mixed[:, lanes]
        scores = dot_nt(query, key) * 0.125 + mask
        probs = jnp.exp(scores - totals[:, lanes][:, :1])
        weighted = probs * dot_nt(upstream, values[:, lanes])
        centred = jnp.sum(weighted, axis=1, keepdims=True)
        d_scores = (weighted - probs * centred).astype(BF)
        d_query.append(jnp.dot(d_scores, key, preferred_element_type=F32) * 0.125)
        d_key.append(dot_tn(d_scores, query) * 0.125)
        d_value.append(dot_tn(probs.astype(BF), upstream))
    dq_ref[...] = jnp.concatenate(d_query, axis=1).astype(BF)
    rows = dq_ref.shape[0]
    for at, parts in enumerate((d_key, d_value)):
        whole = jnp.concatenate(parts, axis=1).astype(BF)
        keep_ref[0, at] = whole[:rows]
        send_ref[0, at] = whole[rows : 2 * rows]
        keep_ref[1, at] = whole[2 * rows : 3 * rows]
        send_ref[1, at] = whole[3 * rows :]


def pair_spec(rows):
    return pl.BlockSpec((rows, 2 * HEAD), lambda at: (0, at))


def attend_forward(queries, keys, values, mask):
    rows, length = mask.shape
    return pl.pallas_call(
        attend_forward_kernel,
        grid=((HEADS + 1) // 2,),
        out_shape=(
            jax.ShapeDtypeStruct((rows, D), BF),
            jax.ShapeDtypeStruct((rows, D), F32),
        ),
        in_specs=[
            pair_spec(rows),
            pair_spec(length),
            pair_spec(length),
            pl.BlockSpec(mask.shape, lambda at: (0, 0)),
        ],
        out_specs=(pair_spec(rows), pair_spec(rows)),
        compiler_params=pltpu.CompilerParams(vmem_limit_bytes=32 * 2**20),
        cost_estimate=pl.CostEstimate(
            flops=4 * rows * length * D,
            bytes_accessed=24 * rows * D,
            transcendentals=HEADS * rows * length,
        ),
    )(queries, keys, values, mask)


def attend_backward(queries, keys, values, mask, totals, d_mixed):
    rows, length = mask.shape
    both = jax.ShapeDtypeStruct((2, 2, rows, D), BF)
    both_spec = pl.BlockSpec((2, 2, rows, 2 * HEAD), lambda at: (0, 0, 0, at))
    return pl.pallas_call(
        attend_backward_kernel,
        grid=((HEADS + 1) // 2,),
        out_shape=(jax.ShapeDtypeStruct((rows, D), BF), both, both),
        in_specs=[
            pair_spec(rows),
            pair_spec(length),
            pair_spec(length),
            pl.BlockSpec(mask.shape, lambda at: (0, 0)),
            pair_spec(rows),
            pair_spec(rows),
        ],
        out_specs=(pair_spec(rows), both_spec, both_spec),
        compiler_params=pltpu.CompilerParams(vmem_limit_bytes=32 * 2**20),
        cost_estimate=pl.CostEstimate(
            flops=10 * rows * length * D,
            bytes_accessed=48 * rows * D,
            transcendentals=HEADS * rows * length,
        ),
    )(queries, keys, values, mask, totals, d_mixed)


def weight_grad_kernel(left_ref, right_ref, out_ref):
    left = left_ref[0]
    pieces = left.shape[1] // SLICE
    empty = jnp.zeros((PAD - SLICE, D), BF)
    for at in range(right_ref.shape[1] // D):
        product = lax.dot_general(
            left,
            right_ref[:, at * D : (at + 1) * D],
            (((0,), (0,)), ((), ())),
            preferred_element_type=F32,
        )
        for piece in range(pieces):
            part = product[piece * SLICE : (piece + 1) * SLICE].astype(BF)
            out_ref[at * pieces + piece, 0] = jnp.concatenate([part, empty])


def weight_grad(left, right):
    _, tokens, width = left.shape
    pieces = right.shape[1] // D * (width // SLICE)
    return pl.pallas_call(
        weight_grad_kernel,
        grid=(2,),
        out_shape=jax.ShapeDtypeStruct((pieces, 2, PAD, D), BF),
        in_specs=[
            pl.BlockSpec((1, tokens, width), lambda at: (at, 0, 0)),
            pl.BlockSpec(right.shape, lambda at: (0, 0)),
        ],
        out_specs=pl.BlockSpec((pieces, 1, PAD, D), lambda at: (0, at, 0, 0)),
        compiler_params=pltpu.CompilerParams(vmem_limit_bytes=48 * 2**20),
        cost_estimate=pl.CostEstimate(
            flops=4 * tokens * width * right.shape[1],
            bytes_accessed=2 * left.size + 2 * right.size + 2 * pieces * 2 * PAD * D,
            transcendentals=0,
        ),
    )(left, right)


def unpack_kernel(in_ref, out_ref):
    count, across = out_ref.shape[0] // SLICE, out_ref.shape[1] // D
    for at in range(across):
        for piece in range(count):
            part = in_ref[at * count + piece].astype(F32)[:SLICE]
            out_ref[piece * SLICE : (piece + 1) * SLICE, at * D : (at + 1) * D] = part


def unpack(pieces, rows):
    columns = pieces.shape[0] * SLICE // rows * D
    return pl.pallas_call(
        unpack_kernel,
        out_shape=jax.ShapeDtypeStruct((rows, columns), F32),
        in_specs=[pl.BlockSpec(memory_space=pltpu.VMEM)],
        out_specs=pl.BlockSpec(memory_space=pltpu.VMEM),
        compiler_params=pltpu.CompilerParams(vmem_limit_bytes=24 * 2**20),
        cost_estimate=pl.CostEstimate(
            flops=0, bytes_accessed=pieces.size * 6, transcendentals=0
        ),
    )(pieces)


def gather_direct(shard):
    far = swap_far(shard)
    return shard, swap_core(shard), far, swap_core(far)


def swap_pair(x, axis):
    return lax.ppermute(x, axis, [(0, 1), (1, 0), (2, 3), (3, 2)])


def gather_quarters(shard):
    across, down = lax.axis_index("x") % 2, lax.axis_index("y") % 2
    quarter = down * 2 + across
    main = shard[:256].reshape(4, 64, shard.shape[1])
    piece = lax.dynamic_index_in_dim(main, quarter, 0, keepdims=False)
    got = swap_far(jnp.concatenate([piece, shard[256:]]))
    mine, rest = got[:64], got[64:]
    by_x, by_y = swap_pair(mine, "x"), swap_pair(mine, "y")
    last = jnp.concatenate([swap_pair(by_y[:32], "x"), swap_pair(by_x[32:], "y")])
    pieces = [mine, by_x, by_y, last]
    return pieces + [rest], [swap_core(piece) for piece in pieces] + [swap_core(rest)]


def gather_spread(shard, spot):
    unit = shard.shape[0] // 17
    main = shard[: 16 * unit].reshape(16, unit, shard.shape[1])
    tail = shard[16 * unit :]
    piece = lax.dynamic_index_in_dim(main, spot, 0, keepdims=False)
    got = swap_far(jnp.concatenate([piece, tail]))
    far = lax.all_gather(got[:unit], ("y", "x"), axis=0, tiled=True)
    rest = got[unit:]
    rows, main = shard.shape[0], 16 * unit
    return assemble(
        rows,
        (shard, swap_core(shard), far, rest, swap_core(far), swap_core(rest)),
        (
            (0, 0, None, rows),
            (1, 0, None, rows),
            (2, 0, None, main),
            (2, main, None, unit),
            (3, 0, None, main),
            (3, main, None, unit),
        ),
    )


def body(
    block_input,
    segment_ids,
    attn_gain,
    attn_shift,
    w_qkv,
    bias_query,
    bias_value,
    w_out,
    bias_out,
    mlp_gain,
    mlp_shift,
    w_up,
    bias_up,
    w_down,
    bias_down,
    cotangent,
):
    core, zh = lax.axis_index("c"), lax.axis_index("zh")
    rank = zh * 2 + core
    spot = lax.axis_index("y") * 4 + lax.axis_index("x")
    small = jnp.concatenate(
        [
            attn_gain,
            attn_shift,
            bias_query,
            bias_value,
            bias_out,
            mlp_gain,
            mlp_shift,
            bias_up,
            bias_down,
        ]
    )
    small = jnp.pad(small[None], ((0, 15), (0, 0)))
    rows = block_input.shape[1]
    own_tokens = block_input[0]
    with_small = jnp.concatenate([w_qkv, small])
    far_parts, across_parts = gather_quarters(with_small)
    beside = swap_core(with_small)
    half_tokens = swap_half(own_tokens)
    tokens = [own_tokens, swap_core(own_tokens), half_tokens, swap_core(half_tokens)]
    turns = [(0, 0, 64), (0, 1, 64), (0, 2, 64), (0, 3, 64), (256, None, 16)]
    full_qkv = assemble(
        QUART,
        (with_small, beside, *far_parts, *across_parts),
        ((0, 0, None, QUART), (1, 0, None, QUART))
        + tuple((2, *turn) for turn in turns)
        + tuple((3, *turn) for turn in turns),
    )
    smalls = [
        value.astype(F32) for value in (small[0], beside[QUART], far_parts[4][16], across_parts[4][16])
    ]
    full_out = assemble(
        QUART, gather_direct(w_out), tuple((flip, 0, None, QUART) for flip in range(4))
    )
    full_up = gather_spread(w_up, spot)
    full_down = gather_spread(w_down, spot)

    ordered = []
    for index in range(4):
        value = smalls[index]
        for at in range(1, 4):
            value = jnp.where(rank == at, smalls[index ^ at], value)
        ordered.append(value)
    ordered = jnp.stack(ordered)

    def vector(start, size):
        return ordered[:, start : start + size].reshape(-1)

    gain_one, shift_one, query_bias, value_bias, out_bias, gain_two, shift_two = (
        vector(QUART * index, QUART) for index in range(7)
    )
    up_bias = vector(7 * QUART, D)
    down_bias = vector(11 * QUART, QUART)

    segments = segment_ids[0]
    upstream = cotangent[0]

    hidden_in = own_tokens.astype(F32)
    normed_parts = [
        layer_norm(part.astype(F32), gain_one, shift_one).astype(BF) for part in tokens
    ]
    normed = normed_parts[0]
    normed_all = jnp.concatenate(normed_parts)
    queries = (
        jnp.dot(normed, full_qkv[:, :D], preferred_element_type=F32) + query_bias
    ).astype(BF)
    keys = jnp.dot(normed_all, full_qkv[:, D : 2 * D], preferred_element_type=F32).astype(BF)
    values = jnp.dot(normed_all, full_qkv[:, 2 * D :], preferred_element_type=F32)
    values = (values + value_bias).astype(BF)
    query_places = rank * rows + jnp.arange(rows)
    starts = [jnp.bitwise_xor(rank, flip) * rows for flip in range(4)]
    key_places = jnp.concatenate([start + jnp.arange(rows) for start in starts])
    key_segments = jnp.concatenate(
        [lax.dynamic_slice_in_dim(segments, start, rows) for start in starts]
    )
    allowed = (key_segments[:rows, None] == key_segments[None, :]) & (
        query_places[:, None] >= key_places[None, :]
    )
    mask = jnp.where(allowed, 0.0, -1e30).astype(F32)
    mixed, log_total = attend_forward(queries, keys, values, mask)
    middle = hidden_in + jnp.dot(mixed, full_out, preferred_element_type=F32) + out_bias
    normed_two = layer_norm(middle, gain_two, shift_two).astype(BF)
    upper = jnp.dot(normed_two, full_up, preferred_element_type=F32) + up_bias
    activated = exact_gelu(upper).astype(BF)
    block_output = middle + jnp.dot(activated, full_down, preferred_element_type=F32) + down_bias

    def paired(value):
        return jnp.concatenate([value, swap_core(value)])

    def paired_columns(value):
        width = value.shape[1] // 4
        blocks = [value[:, at * width : (at + 1) * width] for at in range(4)]
        even, odd = jnp.stack([blocks[0], blocks[2]]), jnp.stack([blocks[1], blocks[3]])
        mine = jnp.where(core == 0, even, odd)
        other = jnp.where(core == 0, odd, even)
        return jnp.concatenate([mine, swap_core(other)], axis=1)

    def across(value):
        rest = value.shape[2]
        value = lax.psum_scatter(
            value.reshape(32 * rest, D), ("y", "x"), scatter_dimension=0, tiled=True
        )
        return value.reshape(2, rest, D)

    upstream_wide = upstream.astype(F32)
    upstream_pair = paired(upstream)
    grad_down_bias = jnp.sum(upstream_wide, axis=0)
    down_part = across(weight_grad(paired_columns(activated), upstream_pair))

    d_activated = jnp.dot(upstream, full_down.T, preferred_element_type=F32)
    gelu_back = jax.vjp(exact_gelu, upper)[1]
    d_upper = gelu_back(d_activated)[0].astype(BF)
    grad_up_bias = jnp.sum(d_upper.astype(F32), axis=0)
    grad_up = weight_grad(paired_columns(normed_two), paired(d_upper))
    down_part, grad_up = lax.optimization_barrier((down_part, grad_up))
    up_part = across(grad_up)

    d_normed_two = jnp.dot(d_upper, full_up.T, preferred_element_type=F32)
    norm_two_back = jax.vjp(layer_norm, middle, gain_two, shift_two)[1]
    d_middle_part, grad_gain_two, grad_shift_two = norm_two_back(d_normed_two)
    d_middle = upstream_wide + d_middle_part
    d_attended = d_middle.astype(BF)
    grad_out_bias = jnp.sum(d_attended.astype(F32), axis=0)
    grad_out = weight_grad(paired_columns(mixed), paired(d_attended))

    d_mixed = jnp.dot(d_attended, full_out.T, preferred_element_type=F32).astype(BF)
    d_queries, d_both, d_beside = attend_backward(
        queries, keys, values, mask, log_total, d_mixed
    )
    d_beside = swap_core(d_beside)
    d_half = swap_half((d_both[1].astype(F32) + d_beside[1].astype(F32)).astype(BF))
    d_both = d_both[0].astype(F32) + d_beside[0].astype(F32) + d_half.astype(F32)
    d_both = d_both.astype(BF)
    d_project = jnp.concatenate([d_queries, d_both[0], d_both[1]], axis=1)
    grad_query_bias = jnp.sum(d_queries.astype(F32), axis=0)
    grad_value_bias = jnp.sum(d_both[1].astype(F32), axis=0)
    grad_qkv = weight_grad(paired_columns(normed), paired(d_project))

    d_normed = jnp.dot(d_project, full_qkv.T, preferred_element_type=F32)
    norm_one_back = jax.vjp(layer_norm, hidden_in, gain_one, shift_one)[1]
    d_input_part, grad_gain_one, grad_shift_one = norm_one_back(d_normed)
    grad_input = d_middle + d_input_part

    vectors = jnp.concatenate(
        [
            value.reshape(4, -1)
            for value in (
                grad_gain_one,
                grad_shift_one,
                grad_query_bias,
                grad_value_bias,
                grad_out_bias,
                grad_gain_two,
                grad_shift_two,
                grad_down_bias,
                grad_up_bias,
            )
        ],
        axis=1,
    )
    even, odd = vectors[0::2], vectors[1::2]
    mine = jnp.where(core == 0, even, odd)
    other = jnp.where(core == 0, odd, even)
    mine = (mine + swap_core(other.astype(BF)).astype(F32)).astype(BF)
    mine = mine.reshape(2, 16, VECTOR).transpose(1, 0, 2)[:, :, None]

    grad_attn = jnp.concatenate([grad_qkv, grad_out])
    grad_attn = lax.dynamic_update_slice(grad_attn, mine, (0, 0, SLICE, 0))
    up_part, grad_attn = lax.optimization_barrier((up_part, grad_attn))
    early = depth_sum(jnp.concatenate([down_part, up_part], axis=1), zh)
    attn_part = depth_sum(lax.optimization_barrier(across(grad_attn)), zh)
    parts = lax.all_gather(
        jnp.concatenate([early, attn_part]).reshape(3, PAD, D), ("y", "x"), axis=0, tiled=False
    ).reshape(16, 3, PAD, D)
    grad_down = unpack(parts[:, 0], D)
    grad_up = unpack(parts[:, 1], QUART)
    grad_qkv = unpack(parts[:12, 2], QUART)
    grad_out = unpack(parts[12:, 2], QUART)
    vectors = parts[:, 2, SLICE, :VECTOR].reshape(-1).astype(F32)

    def owned(start, size):
        return vectors[start : start + size]

    return (
        block_output[None],
        grad_input[None],
        owned(0, QUART),
        owned(QUART, QUART),
        grad_qkv,
        owned(2 * QUART, QUART),
        owned(3 * QUART, QUART),
        grad_out,
        owned(4 * QUART, QUART),
        owned(5 * QUART, QUART),
        owned(6 * QUART, QUART),
        grad_up,
        owned(8 * QUART, D),
        grad_down,
        owned(7 * QUART, QUART),
    )


def solution(mesh):
    grid = Mesh(mesh.devices.reshape(4, 4, 2, 2, 2), AXES)
    rep, grp = ("y", "x", "zl"), ("zh", "c")
    tokens = P(rep, grp, None)
    vector, matrix = P(grp), P(grp, None)
    params = (
        vector,
        vector,
        matrix,
        vector,
        vector,
        matrix,
        vector,
        vector,
        vector,
        matrix,
        vector,
        matrix,
        vector,
    )
    return jax.shard_map(
        body,
        mesh=grid,
        in_specs=(tokens, P(rep, None)) + params + (tokens,),
        out_specs=(tokens, tokens) + params,
        check_vma=False,
    )
```

```python
import functools

import jax
import jax.numpy as jnp
from jax import lax
from jax.experimental import pallas as pl
from jax.experimental.layout import Layout, with_layout_constraint
from jax.experimental.pallas import tpu as pltpu
from jax.sharding import Mesh
from jax.sharding import PartitionSpec as P

D = 1088
HEADS = 17
HEAD = 64
QUART = 272
SLICE = 68
PAD = 72
VECTOR = 204
AXES = ("y", "x", "zl", "zh", "c")
BF = jnp.bfloat16
F32 = jnp.float32


def layer_norm(values, gain, shift):
    centre = values - jnp.mean(values, axis=-1, keepdims=True)
    spread = jnp.mean(centre * centre, axis=-1, keepdims=True)
    return centre * lax.rsqrt(spread + 1e-05) * gain + shift


def exact_gelu(values):
    return jax.nn.gelu(values, approximate=False)


def rows_major(x):
    return with_layout_constraint(x, Layout(major_to_minor=tuple(range(x.ndim))))


def permute(x, axis, pairs):
    shape = x.shape
    if shape[-2] % 128 == 0 and shape[-1] % 128 != 0:
        x = x.reshape(-1, 64, shape[-1])
    return rows_major(lax.ppermute(rows_major(x), axis, pairs)).reshape(shape)


def rotate(x, axis, step):
    return permute(x, axis, [(at, (at + step) % 4) for at in range(4)])


def swap_core(x):
    return permute(x, "c", [(0, 1), (1, 0)])


def swap_half(x):
    return permute(x, "zh", [(0, 1), (1, 0)])


def swap_near(x):
    return permute(x, "zl", [(0, 1), (1, 0)])


def swap_far(x):
    return permute(x, ("zl", "zh"), [(0, 3), (3, 0), (1, 2), (2, 1)])


def swap_pair(x, axis):
    return permute(x, axis, [(0, 1), (1, 0), (2, 3), (3, 2)])


def after_kernel(x_ref, done_ref, out_ref):
    pass


def after(x, done):
    done = done.reshape((-1,) + done.shape[-2:])[0, :16, :128]
    return pl.pallas_call(
        after_kernel,
        out_shape=jax.ShapeDtypeStruct(x.shape, x.dtype),
        in_specs=[pl.BlockSpec(memory_space=pl.ANY)] * 2,
        out_specs=pl.BlockSpec(memory_space=pl.ANY),
        input_output_aliases={0: 0},
    )(x, done)


def pick(values, index, dim):
    start = [0] * values.ndim
    start[dim] = index
    size = list(values.shape)
    size[dim] = 1
    part = lax.dynamic_slice(values, start, size, allow_negative_indices=False)
    return part.reshape(size[:dim] + size[dim + 1 :])


def natural(parts, place):
    found = []
    for index in range(4):
        value = parts[index]
        for at in range(1, 4):
            value = jnp.where(place == at, parts[(index - at) % 4], value)
        found.append(value)
    return jnp.stack(found)


def ring_scatter(values, axis, dim):
    place = lax.axis_index(axis)

    def part(step):
        return pick(values, (place + step) & 3, dim)

    got = [rotate(part(step), axis, step) for step in (2, 1, 3)]
    total = part(0).astype(F32)
    for value in got:
        total = total + value.astype(F32)
    return total.astype(BF)


def ring_gather(piece, axis):
    far, behind, ahead = (rotate(piece, axis, step) for step in (2, 1, 3))
    return natural([piece, ahead, far, behind], lax.axis_index(axis))


def depth_sum(values, zh):
    mine = jnp.where(zh == 0, values[0], values[1])
    other = jnp.where(zh == 0, values[1], values[0])
    far, half, near = swap_far(other), swap_half(other), swap_near(mine)
    total = mine.astype(F32) + near.astype(F32) + far.astype(F32) + half.astype(F32)
    return total.astype(BF)


def assemble_kernel(spots, *refs):
    *parts, out, sems = refs
    rows = out.shape[0] // 4
    rank = lax.axis_index("zh") * 2 + lax.axis_index("c")
    quarter = lax.axis_index("y") % 2 * 2 + lax.axis_index("x") % 2
    copies = []
    for which, row, flip, start, turn, size in spots:
        at = jnp.bitwise_xor(rank, flip) * rows + start
        if turn is not None:
            at = at + jnp.bitwise_xor(quarter, turn) * size
        copy = pltpu.make_async_copy(
            parts[which].at[pl.ds(row, size)],
            out.at[pl.ds(pl.multiple_of(at, 16), size)],
            sems.at[len(copies)],
        )
        copy.start()
        copies.append(copy)
    for copy in copies:
        copy.wait()


def assemble(rows, parts, spots):
    columns = parts[0].shape[1]
    return pl.pallas_call(
        functools.partial(assemble_kernel, spots),
        out_shape=jax.ShapeDtypeStruct((rows * 4, columns), BF),
        in_specs=[pl.BlockSpec(memory_space=pltpu.VMEM)] * len(parts),
        out_specs=pl.BlockSpec(memory_space=pl.ANY),
        scratch_shapes=[pltpu.SemaphoreType.DMA((len(spots),))],
        compiler_params=pltpu.CompilerParams(vmem_limit_bytes=24 * 2**20),
        cost_estimate=pl.CostEstimate(
            flops=0, bytes_accessed=rows * columns * 16, transcendentals=0
        ),
    )(*parts)


def dot_nt(left, right):
    return lax.dot_general(left, right, (((1,), (1,)), ((), ())), preferred_element_type=F32)


def dot_tn(left, right):
    return lax.dot_general(left, right, (((0,), (0,)), ((), ())), preferred_element_type=F32)


def attend_forward_kernel(q_ref, k_ref, v_ref, mask_ref, mixed_ref, total_ref):
    mask = mask_ref[...]
    queries, keys, values = q_ref[...], k_ref[...], v_ref[...]
    mixed, totals = [], []
    for head in range(2):
        lanes = slice(head * HEAD, (head + 1) * HEAD)
        scores = dot_nt(queries[:, lanes], keys[:, lanes]) * 0.125 + mask
        highest = jnp.max(scores, axis=1, keepdims=True)
        powers = jnp.exp(scores - highest)
        total = jnp.sum(powers, axis=1, keepdims=True)
        probs = (powers * (1.0 / total)).astype(BF)
        value = jnp.dot(probs, values[:, lanes], preferred_element_type=F32)
        mixed.append(value)
        totals.append(jnp.broadcast_to(highest + jnp.log(total), value.shape))
    mixed_ref[...] = jnp.concatenate(mixed, axis=1).astype(BF)
    total_ref[...] = jnp.concatenate(totals, axis=1)


def attend_backward_kernel(
    q_ref, k_ref, v_ref, mask_ref, total_ref, d_mixed_ref, dq_ref, keep_ref, send_ref
):
    mask = mask_ref[...]
    queries, keys, values = q_ref[...], k_ref[...], v_ref[...]
    totals, d_mixed = total_ref[...], d_mixed_ref[...]
    d_query, d_key, d_value = [], [], []
    for head in range(2):
        lanes = slice(head * HEAD, (head + 1) * HEAD)
        query, key, upstream = queries[:, lanes], keys[:, lanes], d_mixed[:, lanes]
        scores = dot_nt(query, key) * 0.125 + mask
        probs = jnp.exp(scores - totals[:, lanes][:, :1])
        weighted = probs * dot_nt(upstream, values[:, lanes])
        centred = jnp.sum(weighted, axis=1, keepdims=True)
        d_scores = (weighted - probs * centred).astype(BF)
        d_query.append(jnp.dot(d_scores, key, preferred_element_type=F32) * 0.125)
        d_key.append(dot_tn(d_scores, query) * 0.125)
        d_value.append(dot_tn(probs.astype(BF), upstream))
    dq_ref[...] = jnp.concatenate(d_query, axis=1).astype(BF)
    rows = dq_ref.shape[0]
    for at, parts in enumerate((d_key, d_value)):
        whole = jnp.concatenate(parts, axis=1).astype(BF)
        keep_ref[0, at] = whole[:rows]
        send_ref[0, at] = whole[rows : 2 * rows]
        keep_ref[1, at] = whole[2 * rows : 3 * rows]
        send_ref[1, at] = whole[3 * rows :]


def pair_spec(rows):
    return pl.BlockSpec((rows, 2 * HEAD), lambda at: (0, at))


def attend_forward(queries, keys, values, mask):
    rows, length = mask.shape
    return pl.pallas_call(
        attend_forward_kernel,
        grid=((HEADS + 1) // 2,),
        out_shape=(
            jax.ShapeDtypeStruct((rows, D), BF),
            jax.ShapeDtypeStruct((rows, D), F32),
        ),
        in_specs=[
            pair_spec(rows),
            pair_spec(length),
            pair_spec(length),
            pl.BlockSpec(mask.shape, lambda at: (0, 0)),
        ],
        out_specs=(pair_spec(rows), pair_spec(rows)),
        compiler_params=pltpu.CompilerParams(vmem_limit_bytes=32 * 2**20),
        cost_estimate=pl.CostEstimate(
            flops=4 * rows * length * D,
            bytes_accessed=24 * rows * D,
            transcendentals=HEADS * rows * length,
        ),
    )(queries, keys, values, mask)


def attend_backward(queries, keys, values, mask, totals, d_mixed):
    rows, length = mask.shape
    both = jax.ShapeDtypeStruct((2, 2, rows, D), BF)
    both_spec = pl.BlockSpec((2, 2, rows, 2 * HEAD), lambda at: (0, 0, 0, at))
    return pl.pallas_call(
        attend_backward_kernel,
        grid=((HEADS + 1) // 2,),
        out_shape=(jax.ShapeDtypeStruct((rows, D), BF), both, both),
        in_specs=[
            pair_spec(rows),
            pair_spec(length),
            pair_spec(length),
            pl.BlockSpec(mask.shape, lambda at: (0, 0)),
            pair_spec(rows),
            pair_spec(rows),
        ],
        out_specs=(pair_spec(rows), both_spec, both_spec),
        compiler_params=pltpu.CompilerParams(vmem_limit_bytes=32 * 2**20),
        cost_estimate=pl.CostEstimate(
            flops=10 * rows * length * D,
            bytes_accessed=48 * rows * D,
            transcendentals=HEADS * rows * length,
        ),
    )(queries, keys, values, mask, totals, d_mixed)


def weight_grad_kernel(left_ref, right_ref, *refs):
    out_ref = refs[-1]
    left = left_ref[0]
    pieces = left.shape[1] // SLICE
    empty = jnp.zeros((PAD - SLICE, D), BF)
    for at in range(right_ref.shape[1] // D):
        product = dot_tn(left, right_ref[:, at * D : (at + 1) * D])
        for piece in range(pieces):
            part = product[piece * SLICE : (piece + 1) * SLICE].astype(BF)
            out_ref[at * pieces + piece, 0, 0] = jnp.concatenate([part, empty])


def weight_grad(left, right, slots, first, slot, buffer=None):
    _, tokens, width = left.shape
    pieces = right.shape[1] // D * (width // SLICE)
    in_specs = [
        pl.BlockSpec((1, tokens, width), lambda at: (at, 0, 0)),
        pl.BlockSpec(right.shape, lambda at: (0, 0)),
    ]
    more = () if buffer is None else (buffer,)
    return pl.pallas_call(
        weight_grad_kernel,
        grid=(2,),
        out_shape=jax.ShapeDtypeStruct((16, slots, 2, PAD, D), BF),
        in_specs=in_specs + [pl.BlockSpec(memory_space=pl.ANY)] * len(more),
        out_specs=pl.BlockSpec(
            (pieces, 1, 1, PAD, D), lambda at: (first // pieces, slot, at, 0, 0)
        ),
        input_output_aliases={2: 0} if more else {},
        compiler_params=pltpu.CompilerParams(vmem_limit_bytes=48 * 2**20),
        cost_estimate=pl.CostEstimate(
            flops=4 * tokens * width * right.shape[1],
            bytes_accessed=2 * left.size + 2 * right.size + 2 * pieces * 2 * PAD * D,
            transcendentals=0,
        ),
    )(left, right, *more)


def unpack_kernel(in_ref, out_ref):
    count, across = out_ref.shape[0] // SLICE, out_ref.shape[1] // D
    for at in range(across):
        for piece in range(count):
            part = in_ref[at * count + piece].astype(F32)[:SLICE]
            out_ref[piece * SLICE : (piece + 1) * SLICE, at * D : (at + 1) * D] = part


def unpack(pieces, rows):
    columns = pieces.shape[0] * SLICE // rows * D
    return pl.pallas_call(
        unpack_kernel,
        out_shape=jax.ShapeDtypeStruct((rows, columns), F32),
        in_specs=[pl.BlockSpec(memory_space=pltpu.VMEM)],
        out_specs=pl.BlockSpec(memory_space=pltpu.VMEM),
        compiler_params=pltpu.CompilerParams(vmem_limit_bytes=24 * 2**20),
        cost_estimate=pl.CostEstimate(
            flops=0, bytes_accessed=pieces.size * 6, transcendentals=0
        ),
    )(pieces)


def gather_direct(shard):
    far = swap_far(shard)
    return shard, swap_core(shard), far, swap_core(far)


def gather_quarters(shard):
    across, down = lax.axis_index("x") & 1, lax.axis_index("y") & 1
    quarter = down * 2 + across
    main = shard[:256].reshape(4, 64, shard.shape[1])
    piece = pick(main, quarter, 0)
    got = swap_far(jnp.concatenate([piece, shard[256:]]))
    mine = got[:64]
    by_x, by_y = swap_pair(mine, "x"), swap_pair(mine, "y")
    last_x, last_y = swap_pair(by_y[:32], "x"), swap_pair(by_x[32:], "y")
    return got, jnp.concatenate([got, by_x, by_y, last_x, last_y])


def far_piece(shard, spot, done):
    unit = shard.shape[0] // 17
    main = shard[: 16 * unit].reshape(16, unit, shard.shape[1])
    piece = pick(main, spot, 0)
    return swap_far(after(jnp.concatenate([piece, shard[16 * unit :]]), done))


def gather_spread(shard, got):
    unit = shard.shape[0] // 17
    far = rows_major(lax.all_gather(got[:unit], ("y", "x"), axis=0, tiled=True))
    rest = got[unit:]
    rows, main = shard.shape[0], 16 * unit
    return assemble(
        rows,
        (shard, swap_core(shard), far, rest, swap_core(far), swap_core(rest)),
        (
            (0, 0, 0, 0, None, rows),
            (1, 0, 1, 0, None, rows),
            (2, 0, 2, 0, None, main),
            (3, 0, 2, main, None, unit),
            (4, 0, 3, 0, None, main),
            (5, 0, 3, main, None, unit),
        ),
    )


def body(
    block_input,
    segment_ids,
    attn_gain,
    attn_shift,
    w_qkv,
    bias_query,
    bias_value,
    w_out,
    bias_out,
    mlp_gain,
    mlp_shift,
    w_up,
    bias_up,
    w_down,
    bias_down,
    cotangent,
):
    core, zh = lax.axis_index("c"), lax.axis_index("zh")
    rank = zh * 2 + core
    spot = lax.axis_index("y") * 4 + lax.axis_index("x")
    small = jnp.concatenate(
        [
            attn_gain,
            attn_shift,
            bias_query,
            bias_value,
            bias_out,
            mlp_gain,
            mlp_shift,
            bias_up,
            bias_down,
        ]
    )
    small = jnp.pad(small[None], ((0, 15), (0, 0)))
    rows = block_input.shape[1]
    own_tokens = block_input[0]
    with_small = jnp.concatenate([w_qkv, small])
    beside = swap_core(with_small)
    got_qkv, far_parts = gather_quarters(with_small)
    across_parts = swap_core(far_parts)
    half_tokens = swap_half(after(own_tokens, got_qkv))
    tokens = [own_tokens, swap_core(own_tokens), half_tokens, swap_core(half_tokens)]
    got_up = far_piece(w_up, spot, got_qkv)
    got_down = far_piece(w_down, spot, got_up)
    out_parts = gather_direct(after(w_out, got_down))
    full_up = gather_spread(w_up, got_up)
    full_down = gather_spread(w_down, got_down)
    turns = ((0, 0, 0, 64), (96, 0, 1, 64), (160, 0, 2, 64), (224, 0, 3, 64), (64, 256, None, 16))
    full_qkv = assemble(
        QUART,
        (with_small, beside, far_parts, across_parts),
        ((0, 0, 0, 0, None, QUART), (1, 0, 1, 0, None, QUART))
        + tuple((2, row, 2, *turn) for row, *turn in turns)
        + tuple((3, row, 3, *turn) for row, *turn in turns),
    )
    smalls = [
        value.astype(F32) for value in (small[0], beside[QUART], far_parts[80], across_parts[80])
    ]
    full_out = assemble(
        QUART, out_parts, tuple((flip, 0, flip, 0, None, QUART) for flip in range(4))
    )

    ordered = []
    for index in range(4):
        value = smalls[index]
        for at in range(1, 4):
            value = jnp.where(rank == at, smalls[index ^ at], value)
        ordered.append(value)
    ordered = jnp.stack(ordered)

    def vector(start, size):
        return ordered[:, start : start + size].reshape(-1)

    gain_one, shift_one, query_bias, value_bias, out_bias, gain_two, shift_two = (
        vector(QUART * index, QUART) for index in range(7)
    )
    up_bias = vector(7 * QUART, D)
    down_bias = vector(11 * QUART, QUART)

    segments = segment_ids[0]
    upstream = cotangent[0]

    hidden_in = own_tokens.astype(F32)
    normed_parts = [
        layer_norm(part.astype(F32), gain_one, shift_one).astype(BF) for part in tokens
    ]
    normed = normed_parts[0]
    normed_all = jnp.concatenate(normed_parts)
    queries = (
        jnp.dot(normed, full_qkv[:, :D], preferred_element_type=F32) + query_bias
    ).astype(BF)
    keys = jnp.dot(normed_all, full_qkv[:, D : 2 * D], preferred_element_type=F32).astype(BF)
    values = jnp.dot(normed_all, full_qkv[:, 2 * D :], preferred_element_type=F32)
    values = (values + value_bias).astype(BF)
    query_places = rank * rows + jnp.arange(rows)
    starts = [jnp.bitwise_xor(rank, flip) * rows for flip in range(4)]
    key_places = jnp.concatenate([start + jnp.arange(rows) for start in starts])
    key_segments = jnp.concatenate(
        [
            lax.dynamic_slice(segments, (start,), (rows,), allow_negative_indices=False)
            for start in starts
        ]
    )
    allowed = (key_segments[:rows, None] == key_segments[None, :]) & (
        query_places[:, None] >= key_places[None, :]
    )
    mask = jnp.where(allowed, 0.0, -1e30).astype(F32)
    mixed, log_total = attend_forward(queries, keys, values, mask)
    middle = hidden_in + jnp.dot(mixed, full_out, preferred_element_type=F32) + out_bias
    normed_two = layer_norm(middle, gain_two, shift_two).astype(BF)
    upper = jnp.dot(normed_two, full_up, preferred_element_type=F32) + up_bias
    activated = exact_gelu(upper).astype(BF)
    block_output = middle + jnp.dot(activated, full_down, preferred_element_type=F32) + down_bias

    def paired(value):
        return jnp.concatenate([value, swap_core(value)])

    def paired_columns(value):
        width = value.shape[1] // 4
        blocks = [value[:, at * width : (at + 1) * width] for at in range(4)]
        even, odd = jnp.stack([blocks[0], blocks[2]]), jnp.stack([blocks[1], blocks[3]])
        mine = jnp.where(core == 0, even, odd)
        other = jnp.where(core == 0, odd, even)
        return jnp.concatenate([mine, swap_core(other)], axis=1)

    upstream_wide = upstream.astype(F32)
    upstream_pair = paired(upstream)
    grad_down_bias = jnp.sum(upstream_wide, axis=0)
    activated_pair = paired_columns(activated)

    d_activated = jnp.dot(upstream, full_down.T, preferred_element_type=F32)
    gelu_back = jax.vjp(exact_gelu, upper)[1]
    d_upper = gelu_back(d_activated)[0].astype(BF)
    grad_up_bias = jnp.sum(d_upper.astype(F32), axis=0)
    normed_two_pair, d_upper_pair = paired_columns(normed_two), paired(d_upper)
    grad_mlp = weight_grad(activated_pair, upstream_pair, 2, 0, 0)
    grad_mlp = weight_grad(normed_two_pair, d_upper_pair, 2, 0, 1, grad_mlp)
    mlp_part = lax.psum_scatter(
        grad_mlp.reshape(64 * PAD, D), ("y", "x"), scatter_dimension=0, tiled=True
    ).reshape(2, 2, PAD, D)

    d_normed_two = jnp.dot(d_upper, full_up.T, preferred_element_type=F32)
    norm_two_back = jax.vjp(layer_norm, middle, gain_two, shift_two)[1]
    d_middle_part, grad_gain_two, grad_shift_two = norm_two_back(d_normed_two)
    d_middle = upstream_wide + d_middle_part
    d_attended = d_middle.astype(BF)
    grad_out_bias = jnp.sum(d_attended.astype(F32), axis=0)
    mixed_pair, d_attended_pair = paired_columns(mixed), paired(d_attended)
    normed_pair = paired_columns(normed)

    d_mixed = jnp.dot(d_attended, full_out.T, preferred_element_type=F32).astype(BF)
    d_queries, d_both, d_beside = attend_backward(
        queries, keys, values, mask, log_total, after(d_mixed, grad_mlp)
    )
    d_beside = swap_core(d_beside)
    d_half = swap_half((d_both[1].astype(F32) + d_beside[1].astype(F32)).astype(BF))
    d_both = d_both[0].astype(F32) + d_beside[0].astype(F32) + d_half.astype(F32)
    d_both = d_both.astype(BF)
    d_project = jnp.concatenate([d_queries, d_both[0], d_both[1]], axis=1)
    grad_query_bias = jnp.sum(d_queries.astype(F32), axis=0)
    grad_value_bias = jnp.sum(d_both[1].astype(F32), axis=0)
    grad_attn = weight_grad(mixed_pair, d_attended_pair, 1, 12, 0)
    grad_attn = weight_grad(normed_pair, paired(d_project), 1, 0, 0, grad_attn)

    d_normed = jnp.dot(d_project, full_qkv.T, preferred_element_type=F32)
    norm_one_back = jax.vjp(layer_norm, hidden_in, gain_one, shift_one)[1]
    d_input_part, grad_gain_one, grad_shift_one = norm_one_back(d_normed)
    grad_input = d_middle + d_input_part

    vectors = jnp.concatenate(
        [
            value.reshape(4, -1)
            for value in (
                grad_gain_one,
                grad_shift_one,
                grad_query_bias,
                grad_value_bias,
                grad_out_bias,
                grad_gain_two,
                grad_shift_two,
                grad_down_bias,
                grad_up_bias,
            )
        ],
        axis=1,
    )
    even, odd = vectors[0::2], vectors[1::2]
    mine = jnp.where(core == 0, even, odd)
    other = jnp.where(core == 0, odd, even)
    mine = (mine + swap_core(other.astype(BF)).astype(F32)).astype(BF)
    mine = mine.reshape(2, 16, VECTOR).transpose(1, 0, 2)[:, :, None]

    grad_attn = lax.dynamic_update_slice(grad_attn[:, 0], mine, (0, 0, SLICE, 0))
    grad_attn = after(grad_attn, mlp_part)
    one = ring_scatter(grad_attn[:, 0].reshape(4, 4, PAD, D), "x", 1)
    two = ring_scatter(grad_attn[:, 1].reshape(4, 4, PAD, D), "y", 0)
    one, two = ring_scatter(one, "y", 0), ring_scatter(two, "x", 0)
    attn_part = depth_sum(jnp.stack([one, two]), zh)
    one, two = ring_gather(attn_part[:40], "x"), ring_gather(attn_part[40:], "y")
    one, two = ring_gather(one, "y"), ring_gather(two, "x")
    attn = jnp.concatenate([one, two.transpose(1, 0, 2, 3)], axis=2).reshape(16, PAD, D)
    grad_qkv = unpack(attn[:12], QUART)
    grad_out = unpack(attn[12:], QUART)
    vectors = attn[:, SLICE, :VECTOR].reshape(-1).astype(F32)

    early = depth_sum(mlp_part.transpose(1, 0, 2, 3).reshape(2, 2 * PAD, D), zh)
    parts = lax.all_gather(early, ("y", "x"), axis=0, tiled=True).reshape(16, 2, PAD, D)
    grad_down = unpack(parts[:, 0], D)
    grad_up = unpack(parts[:, 1], QUART)

    def owned(start, size):
        return vectors[start : start + size]

    return (
        block_output[None],
        grad_input[None],
        owned(0, QUART),
        owned(QUART, QUART),
        grad_qkv,
        owned(2 * QUART, QUART),
        owned(3 * QUART, QUART),
        grad_out,
        owned(4 * QUART, QUART),
        owned(5 * QUART, QUART),
        owned(6 * QUART, QUART),
        grad_up,
        owned(8 * QUART, D),
        grad_down,
        owned(7 * QUART, QUART),
    )


def solution(mesh):
    grid = Mesh(mesh.devices.reshape(4, 4, 2, 2, 2), AXES)
    rep, grp = ("y", "x", "zl"), ("zh", "c")
    tokens = P(rep, grp, None)
    vector, matrix = P(grp), P(grp, None)
    params = (
        vector,
        vector,
        matrix,
        vector,
        vector,
        matrix,
        vector,
        vector,
        vector,
        matrix,
        vector,
        matrix,
        vector,
    )
    return jax.shard_map(
        body,
        mesh=grid,
        in_specs=(tokens, P(rep, None)) + params + (tokens,),
        out_specs=(tokens, tokens) + params,
        check_vma=False,
    )
```

```python
import functools

import jax
import jax.numpy as jnp
from jax import lax
from jax.experimental import pallas as pl
from jax.experimental.layout import Layout, with_layout_constraint
from jax.experimental.pallas import tpu as pltpu
from jax.sharding import Mesh
from jax.sharding import PartitionSpec as P

D = 1088
HEADS = 17
HEAD = 64
QUART = 272
SLICE = 68
PAD = 72
VECTOR = 272
AXES = ("y", "x", "zl", "zh", "c")
BF = jnp.bfloat16
F32 = jnp.float32


def layer_norm(values, gain, shift):
    centre = values - jnp.mean(values, axis=-1, keepdims=True)
    spread = jnp.mean(centre * centre, axis=-1, keepdims=True)
    return centre * lax.rsqrt(spread + 1e-05) * gain + shift


def gelu_both(values):
    below = 0.5 * (1.0 + lax.erf(values * 0.7071067811865476))
    density = jnp.exp(values * values * -0.5) * 0.3989422804014327
    return values * below, below + values * density


def rows_major(x):
    return with_layout_constraint(x, Layout(major_to_minor=tuple(range(x.ndim))))


def permute(x, axis, pairs):
    shape = x.shape
    if shape[-2] % 128 == 0 and shape[-1] % 128 != 0:
        x = x.reshape(-1, 64, shape[-1])
    return rows_major(lax.ppermute(rows_major(x), axis, pairs)).reshape(shape)


def rotate(x, axis, step):
    return permute(x, axis, [(at, (at + step) % 4) for at in range(4)])


def swap_core(x):
    return permute(x, "c", [(0, 1), (1, 0)])


def swap_half(x):
    return permute(x, "zh", [(0, 1), (1, 0)])


def swap_near(x):
    return permute(x, "zl", [(0, 1), (1, 0)])


def swap_far(x):
    return permute(x, ("zl", "zh"), [(0, 3), (3, 0), (1, 2), (2, 1)])


def swap_pair(x, axis):
    return permute(x, axis, [(0, 1), (1, 0), (2, 3), (3, 2)])


def after_kernel(x_ref, done_ref, out_ref):
    pass


def after(x, done):
    done = done.reshape((-1,) + done.shape[-2:])[0, :16, :128]
    return pl.pallas_call(
        after_kernel,
        out_shape=jax.ShapeDtypeStruct(x.shape, x.dtype),
        in_specs=[pl.BlockSpec(memory_space=pl.ANY)] * 2,
        out_specs=pl.BlockSpec(memory_space=pl.ANY),
        input_output_aliases={0: 0},
    )(x, done)


def rows_of(values, start, size):
    return lax.dynamic_slice(
        values, (start, 0), (size, values.shape[1]), allow_negative_indices=False
    )


def natural(parts, place):
    found = []
    for index in range(4):
        value = parts[index]
        for at in range(1, 4):
            value = jnp.where(place == at, parts[(index - at) % 4], value)
        found.append(value)
    return jnp.stack(found)


def ring_scatter(part, axis):
    place = lax.axis_index(axis)
    got = [rotate(part((place + step) & 3), axis, step) for step in (2, 1, 3)]
    total = part(place).astype(F32)
    for value in got:
        total = total + value.astype(F32)
    return total.astype(BF)


def ring_gather(piece, axis):
    far, behind, ahead = (rotate(piece, axis, step) for step in (2, 1, 3))
    return natural([piece, ahead, far, behind], lax.axis_index(axis))


def depth_sum(values, zh):
    mine = jnp.where(zh == 0, values[0], values[1])
    other = jnp.where(zh == 0, values[1], values[0])
    far, half, near = swap_far(other), swap_half(other), swap_near(mine)
    total = mine.astype(F32) + near.astype(F32) + far.astype(F32) + half.astype(F32)
    return total.astype(BF)


def assemble_kernel(spots, *refs):
    *parts, out, sems = refs
    rows = out.shape[0] // 4
    rank = lax.axis_index("zh") * 2 + lax.axis_index("c")
    quarter = lax.axis_index("y") % 2 * 2 + lax.axis_index("x") % 2
    copies = []
    for which, row, flip, start, turn, size in spots:
        at = jnp.bitwise_xor(rank, flip) * rows + start
        if turn is not None:
            at = at + jnp.bitwise_xor(quarter, turn) * size
        copy = pltpu.make_async_copy(
            parts[which].at[pl.ds(row, size)],
            out.at[pl.ds(pl.multiple_of(at, 16), size)],
            sems.at[len(copies)],
        )
        copy.start()
        copies.append(copy)
    for copy in copies:
        copy.wait()


def assemble(rows, parts, spots):
    columns = parts[0].shape[1]
    return pl.pallas_call(
        functools.partial(assemble_kernel, spots),
        out_shape=jax.ShapeDtypeStruct((rows * 4, columns), BF),
        in_specs=[pl.BlockSpec(memory_space=pltpu.VMEM)] * len(parts),
        out_specs=pl.BlockSpec(memory_space=pl.ANY),
        scratch_shapes=[pltpu.SemaphoreType.DMA((len(spots),))],
        compiler_params=pltpu.CompilerParams(vmem_limit_bytes=24 * 2**20),
        cost_estimate=pl.CostEstimate(
            flops=0, bytes_accessed=rows * columns * 16, transcendentals=0
        ),
    )(*parts)


def dot_nt(left, right):
    return lax.dot_general(left, right, (((1,), (1,)), ((), ())), preferred_element_type=F32)


def dot_tn(left, right):
    return lax.dot_general(left, right, (((0,), (0,)), ((), ())), preferred_element_type=F32)


def attend_forward_kernel(q_ref, k_ref, v_ref, mask_ref, mixed_ref, total_ref):
    mask = mask_ref[...]
    queries, keys, values = q_ref[...], k_ref[...], v_ref[...]
    mixed, totals = [], []
    for head in range(2):
        lanes = slice(head * HEAD, (head + 1) * HEAD)
        scores = dot_nt(queries[:, lanes], keys[:, lanes]) * 0.125 + mask
        highest = jnp.max(scores, axis=1, keepdims=True)
        powers = jnp.exp(scores - highest)
        total = jnp.sum(powers, axis=1, keepdims=True)
        probs = (powers * (1.0 / total)).astype(BF)
        value = jnp.dot(probs, values[:, lanes], preferred_element_type=F32)
        mixed.append(value)
        totals.append(jnp.broadcast_to(highest + jnp.log(total), value.shape))
    mixed_ref[...] = jnp.concatenate(mixed, axis=1).astype(BF)
    total_ref[...] = jnp.concatenate(totals, axis=1)


def attend_backward_kernel(
    q_ref, k_ref, v_ref, mask_ref, total_ref, d_mixed_ref, dq_ref, keep_ref, send_ref
):
    mask = mask_ref[...]
    queries, keys, values = q_ref[...], k_ref[...], v_ref[...]
    totals, d_mixed = total_ref[...], d_mixed_ref[...]
    d_query, d_key, d_value = [], [], []
    for head in range(2):
        lanes = slice(head * HEAD, (head + 1) * HEAD)
        query, key, upstream = queries[:, lanes], keys[:, lanes], d_mixed[:, lanes]
        scores = dot_nt(query, key) * 0.125 + mask
        probs = jnp.exp(scores - totals[:, lanes][:, :1])
        weighted = probs * dot_nt(upstream, values[:, lanes])
        centred = jnp.sum(weighted, axis=1, keepdims=True)
        d_scores = (weighted - probs * centred).astype(BF)
        d_query.append(jnp.dot(d_scores, key, preferred_element_type=F32) * 0.125)
        d_key.append(dot_tn(d_scores, query) * 0.125)
        d_value.append(dot_tn(probs.astype(BF), upstream))
    dq_ref[...] = jnp.concatenate(d_query, axis=1).astype(BF)
    rows = dq_ref.shape[0]
    for at, parts in enumerate((d_key, d_value)):
        whole = jnp.concatenate(parts, axis=1).astype(BF)
        keep_ref[0, at] = whole[:rows]
        send_ref[0, at] = whole[rows : 2 * rows]
        keep_ref[1, at] = whole[2 * rows : 3 * rows]
        send_ref[1, at] = whole[3 * rows :]


def pair_spec(rows):
    return pl.BlockSpec((rows, 2 * HEAD), lambda at: (0, at))


def attend_forward(queries, keys, values, mask):
    rows, length = mask.shape
    return pl.pallas_call(
        attend_forward_kernel,
        grid=((HEADS + 1) // 2,),
        out_shape=(
            jax.ShapeDtypeStruct((rows, D), BF),
            jax.ShapeDtypeStruct((rows, D), F32),
        ),
        in_specs=[
            pair_spec(rows),
            pair_spec(length),
            pair_spec(length),
            pl.BlockSpec(mask.shape, lambda at: (0, 0)),
        ],
        out_specs=(pair_spec(rows), pair_spec(rows)),
        compiler_params=pltpu.CompilerParams(vmem_limit_bytes=32 * 2**20),
        cost_estimate=pl.CostEstimate(
            flops=4 * rows * length * D,
            bytes_accessed=24 * rows * D,
            transcendentals=HEADS * rows * length,
        ),
    )(queries, keys, values, mask)


def attend_backward(queries, keys, values, mask, totals, d_mixed):
    rows, length = mask.shape
    both = jax.ShapeDtypeStruct((2, 2, rows, D), BF)
    both_spec = pl.BlockSpec((2, 2, rows, 2 * HEAD), lambda at: (0, 0, 0, at))
    return pl.pallas_call(
        attend_backward_kernel,
        grid=((HEADS + 1) // 2,),
        out_shape=(jax.ShapeDtypeStruct((rows, D), BF), both, both),
        in_specs=[
            pair_spec(rows),
            pair_spec(length),
            pair_spec(length),
            pl.BlockSpec(mask.shape, lambda at: (0, 0)),
            pair_spec(rows),
            pair_spec(rows),
        ],
        out_specs=(pair_spec(rows), both_spec, both_spec),
        compiler_params=pltpu.CompilerParams(vmem_limit_bytes=32 * 2**20),
        cost_estimate=pl.CostEstimate(
            flops=10 * rows * length * D,
            bytes_accessed=48 * rows * D,
            transcendentals=HEADS * rows * length,
        ),
    )(queries, keys, values, mask, totals, d_mixed)


def weight_grad_kernel(count, first, *refs):
    lefts, rights = refs[:2], refs[2 : 2 + 2 * count]
    vector_ref, out_ref = refs[2 + 2 * count], refs[-1]
    left, left_other = lefts[0][0], lefts[1][0]
    pieces = left.shape[1] // SLICE
    done = 0
    for own, other in zip(rights[::2], rights[1::2]):
        for at in range(own.shape[-1] // D):
            lanes = slice(at * D, (at + 1) * D)
            product = dot_tn(left, own[:, lanes]) + dot_tn(left_other, other[:, lanes])
            for piece in range(pieces):
                part = product[piece * SLICE : (piece + 1) * SLICE]
                empty = jnp.zeros((PAD - SLICE, D), F32)
                if first == 0 and count == 3:
                    row = vector_ref[0, done : done + 1]
                    empty = jnp.concatenate([row, empty[1:]])
                out_ref[done, 0, 0] = jnp.concatenate([part, empty]).astype(BF)
                done += 1


def weight_grad(lefts, rights, vectors, slots, first, slot, buffer=None):
    _, tokens, width = lefts[0].shape
    rights = [value for pair in rights for value in pair]
    blocks = sum(value.shape[1] for value in rights[::2]) // D
    pieces = blocks * (width // SLICE)
    in_specs = [pl.BlockSpec((1, tokens, width), lambda at: (at, 0, 0))] * 2
    in_specs += [pl.BlockSpec(value.shape, lambda at: (0, 0)) for value in rights]
    in_specs += [pl.BlockSpec((1,) + vectors.shape[1:], lambda at: (at, 0, 0))]
    more = () if buffer is None else (buffer,)
    operands = (*lefts, *rights, vectors)
    return pl.pallas_call(
        functools.partial(weight_grad_kernel, len(rights) // 2, first),
        grid=(2,),
        out_shape=jax.ShapeDtypeStruct((16, slots, 2, PAD, D), BF),
        in_specs=in_specs + [pl.BlockSpec(memory_space=pl.ANY)] * len(more),
        out_specs=pl.BlockSpec(
            (pieces, 1, 1, PAD, D), lambda at: (first // pieces, slot, at, 0, 0)
        ),
        input_output_aliases={len(operands): 0} if more else {},
        compiler_params=pltpu.CompilerParams(vmem_limit_bytes=48 * 2**20),
        cost_estimate=pl.CostEstimate(
            flops=8 * tokens * width * blocks * D,
            bytes_accessed=2 * sum(value.size for value in operands) + 4 * pieces * PAD * D,
            transcendentals=0,
        ),
    )(*operands, *more)


def unpack_kernel(in_ref, out_ref):
    count, across = out_ref.shape[0] // SLICE, out_ref.shape[1] // D
    for at in range(across):
        for piece in range(count):
            part = in_ref[at * count + piece].astype(F32)[:SLICE]
            out_ref[piece * SLICE : (piece + 1) * SLICE, at * D : (at + 1) * D] = part


def unpack(pieces, rows):
    columns = pieces.shape[0] * SLICE // rows * D
    return pl.pallas_call(
        unpack_kernel,
        out_shape=jax.ShapeDtypeStruct((rows, columns), F32),
        in_specs=[pl.BlockSpec(memory_space=pltpu.VMEM)],
        out_specs=pl.BlockSpec(memory_space=pltpu.VMEM),
        compiler_params=pltpu.CompilerParams(vmem_limit_bytes=24 * 2**20),
        cost_estimate=pl.CostEstimate(
            flops=0, bytes_accessed=pieces.size * 6, transcendentals=0
        ),
    )(pieces)


def gather_quarters(shard, small):
    across, down = lax.axis_index("x") & 1, lax.axis_index("y") & 1
    quarter = down * 2 + across
    piece = rows_of(shard, quarter * 64, 64)
    got = swap_far(jnp.concatenate([piece, shard[256:], small]))
    mine = got[:64]
    by_x, by_y = swap_pair(mine, "x"), swap_pair(mine, "y")
    last_x, last_y = swap_pair(by_y[:32], "x"), swap_pair(by_x[32:], "y")
    return by_x, jnp.concatenate([got, by_x, by_y, last_x, last_y])


def far_piece(shard, spot, done):
    unit = shard.shape[0] // 17
    piece = rows_of(shard, spot * unit, unit)
    return swap_far(after(jnp.concatenate([piece, shard[16 * unit :]]), done))


def gather_spread(shard, got):
    unit = shard.shape[0] // 17
    far = rows_major(lax.all_gather(got[:unit], ("y", "x"), axis=0, tiled=True))
    rest = got[unit:]
    rows, main = shard.shape[0], 16 * unit
    return assemble(
        rows,
        (shard, swap_core(shard), far, rest, swap_core(far), swap_core(rest)),
        (
            (0, 0, 0, 0, None, rows),
            (1, 0, 1, 0, None, rows),
            (2, 0, 2, 0, None, main),
            (3, 0, 2, main, None, unit),
            (4, 0, 3, 0, None, main),
            (5, 0, 3, main, None, unit),
        ),
    )


def body(
    block_input,
    segment_ids,
    attn_gain,
    attn_shift,
    w_qkv,
    bias_query,
    bias_value,
    w_out,
    bias_out,
    mlp_gain,
    mlp_shift,
    w_up,
    bias_up,
    w_down,
    bias_down,
    cotangent,
):
    core, zh = lax.axis_index("c"), lax.axis_index("zh")
    rank = zh * 2 + core
    spot = lax.axis_index("y") * 4 + lax.axis_index("x")
    small = jnp.concatenate(
        [
            attn_gain,
            attn_shift,
            bias_query,
            bias_value,
            bias_out,
            mlp_gain,
            mlp_shift,
            bias_up,
            bias_down,
        ]
    )
    small = jnp.pad(small[None], ((0, 15), (0, 0)))
    rows = block_input.shape[1]
    own_tokens = block_input[0]
    by_x, far_parts = gather_quarters(w_qkv, small)
    beside = swap_core(jnp.concatenate([w_qkv, small]))
    across_parts = swap_core(far_parts)
    half_tokens = swap_half(after(own_tokens, by_x))
    tokens = [own_tokens, swap_core(own_tokens), half_tokens, swap_core(half_tokens)]
    got_up = far_piece(w_up, spot, by_x)
    got_down = far_piece(w_down, spot, got_up)
    full_up = gather_spread(w_up, got_up)
    full_down = gather_spread(w_down, got_down)
    turns = ((0, 0, 0, 64), (96, 0, 1, 64), (160, 0, 2, 64), (224, 0, 3, 64), (64, 256, None, 16))
    full_qkv = assemble(
        QUART,
        (w_qkv, beside, far_parts, across_parts),
        ((0, 0, 0, 0, None, QUART), (1, 0, 1, 0, None, QUART))
        + tuple((2, row, 2, *turn) for row, *turn in turns)
        + tuple((3, row, 3, *turn) for row, *turn in turns),
    )
    smalls = [
        value.astype(F32) for value in (small[0], beside[QUART], far_parts[80], across_parts[80])
    ]
    far_out = after(swap_far(after(w_out, got_down)), full_qkv)
    full_out = assemble(
        QUART,
        (w_out, swap_core(w_out), far_out, swap_core(far_out)),
        tuple((flip, 0, flip, 0, None, QUART) for flip in range(4)),
    )

    ordered = []
    for index in range(4):
        value = smalls[index]
        for at in range(1, 4):
            value = jnp.where(rank == at, smalls[index ^ at], value)
        ordered.append(value)
    ordered = jnp.stack(ordered)

    def vector(start, size):
        return ordered[:, start : start + size].reshape(-1)

    gain_one, shift_one, query_bias, value_bias, out_bias, gain_two, shift_two = (
        vector(QUART * index, QUART) for index in range(7)
    )
    up_bias = vector(7 * QUART, D)
    down_bias = vector(11 * QUART, QUART)

    segments = segment_ids[0]
    upstream = cotangent[0]

    hidden_in = own_tokens.astype(F32)
    normed_parts = [
        layer_norm(part.astype(F32), gain_one, shift_one).astype(BF) for part in tokens
    ]
    normed = normed_parts[0]
    normed_all = jnp.concatenate(normed_parts)
    queries = (
        jnp.dot(normed, full_qkv[:, :D], preferred_element_type=F32) + query_bias
    ).astype(BF)
    keys = jnp.dot(normed_all, full_qkv[:, D : 2 * D], preferred_element_type=F32).astype(BF)
    values = jnp.dot(normed_all, full_qkv[:, 2 * D :], preferred_element_type=F32)
    values = (values + value_bias).astype(BF)
    query_places = rank * rows + jnp.arange(rows)
    starts = [jnp.bitwise_xor(rank, flip) * rows for flip in range(4)]
    key_places = jnp.concatenate([start + jnp.arange(rows) for start in starts])
    key_segments = jnp.concatenate(
        [
            lax.dynamic_slice(segments, (start,), (rows,), allow_negative_indices=False)
            for start in starts
        ]
    )
    allowed = (key_segments[:rows, None] == key_segments[None, :]) & (
        query_places[:, None] >= key_places[None, :]
    )
    mask = jnp.where(allowed, 0.0, -1e30).astype(F32)
    mixed, log_total = attend_forward(queries, keys, values, mask)
    middle = hidden_in + jnp.dot(mixed, full_out, preferred_element_type=F32) + out_bias
    normed_two = layer_norm(middle, gain_two, shift_two).astype(BF)
    upper = jnp.dot(normed_two, full_up, preferred_element_type=F32) + up_bias
    activated, slope = gelu_both(upper)
    activated = activated.astype(BF)
    block_output = middle + jnp.dot(activated, full_down, preferred_element_type=F32) + down_bias

    def paired(value):
        return value, swap_core(value)

    def paired_columns(value):
        width = value.shape[1] // 4
        blocks = [value[:, at * width : (at + 1) * width] for at in range(4)]
        even, odd = jnp.stack([blocks[0], blocks[2]]), jnp.stack([blocks[1], blocks[3]])
        mine = jnp.where(core == 0, even, odd)
        other = jnp.where(core == 0, odd, even)
        return mine, swap_core(other)

    upstream_wide = upstream.astype(F32)
    upstream_pair = paired(upstream)
    grad_down_bias = jnp.sum(upstream_wide, axis=0)
    activated_pair = paired_columns(activated)

    d_activated = jnp.dot(upstream, full_down.T, preferred_element_type=F32)
    d_upper = (d_activated * slope).astype(BF)
    grad_up_bias = jnp.sum(d_upper.astype(F32), axis=0)
    normed_two_pair, d_upper_pair = paired_columns(normed_two), paired(d_upper)
    no_vectors = jnp.zeros((2, 12, D), F32)
    grad_mlp = weight_grad(activated_pair, [upstream_pair], no_vectors, 2, 0, 0)
    grad_mlp = weight_grad(
        normed_two_pair, [d_upper_pair], no_vectors, 2, 0, 1, grad_mlp
    )
    mlp_part = lax.psum_scatter(
        grad_mlp.reshape(64 * PAD, D), ("y", "x"), scatter_dimension=0, tiled=True
    ).reshape(2, 2, PAD, D)

    d_normed_two = jnp.dot(d_upper, full_up.T, preferred_element_type=F32)
    norm_two_back = jax.vjp(layer_norm, middle, gain_two, shift_two)[1]
    d_middle_part, grad_gain_two, grad_shift_two = norm_two_back(d_normed_two)
    d_middle = upstream_wide + d_middle_part
    d_attended = d_middle.astype(BF)
    grad_out_bias = jnp.sum(d_attended.astype(F32), axis=0)
    mixed_pair, d_attended_pair = paired_columns(mixed), paired(d_attended)
    normed_pair = paired_columns(normed)

    d_mixed = jnp.dot(d_attended, full_out.T, preferred_element_type=F32).astype(BF)
    d_queries, d_both, d_beside = attend_backward(
        queries, keys, values, mask, log_total, after(d_mixed, grad_mlp)
    )
    d_beside = swap_core(d_beside)
    d_half = swap_half((d_both[1].astype(F32) + d_beside[1].astype(F32)).astype(BF))
    d_both = d_both[0].astype(F32) + d_beside[0].astype(F32) + d_half.astype(F32)
    d_both = d_both.astype(BF)
    d_keys, d_values = d_both[0], d_both[1]
    grad_query_bias = jnp.sum(d_queries.astype(F32), axis=0)
    grad_value_bias = jnp.sum(d_values.astype(F32), axis=0)
    rights = [paired(d_queries), paired(d_keys), paired(d_values)]
    d_normed = None
    for at, part in enumerate((d_queries, d_keys, d_values)):
        term = lax.dot_general(
            part,
            full_qkv[:, at * D : (at + 1) * D],
            (((1,), (1,)), ((), ())),
            preferred_element_type=F32,
        )
        d_normed = term if d_normed is None else d_normed + term
    norm_one_back = jax.vjp(layer_norm, hidden_in, gain_one, shift_one)[1]
    d_input_part, grad_gain_one, grad_shift_one = norm_one_back(d_normed)
    grad_input = d_middle + d_input_part

    vectors = jnp.concatenate(
        [
            value.reshape(4, -1)
            for value in (
                grad_gain_one,
                grad_shift_one,
                grad_query_bias,
                grad_value_bias,
                grad_out_bias,
                grad_gain_two,
                grad_shift_two,
                grad_down_bias,
                grad_up_bias,
            )
        ],
        axis=1,
    )
    even, odd = vectors[0::2], vectors[1::2]
    mine = jnp.where(core == 0, even, odd)
    other = jnp.where(core == 0, odd, even)
    mine = (mine + swap_core(other.astype(BF)).astype(F32)).astype(BF)
    mine = jnp.pad(mine.reshape(2, 12, VECTOR).astype(F32), ((0, 0), (0, 0), (0, D - VECTOR)))

    early = depth_sum(mlp_part.transpose(1, 0, 2, 3).reshape(2, 2 * PAD, D), zh)
    normed_pair = (normed_pair[0], after(normed_pair[1], early))
    grad_attn = weight_grad(mixed_pair, [d_attended_pair], no_vectors, 1, 12, 0)
    grad_attn = weight_grad(normed_pair, rights, mine, 1, 0, 0, grad_attn)
    grad_attn = grad_attn.reshape(4, 4, 2, PAD, D)

    def cut(start, size):
        return lax.dynamic_slice(grad_attn, start, size, allow_negative_indices=False)

    def part_of(values):
        return lambda place: cut_row(values, place)

    def cut_row(values, place):
        return lax.dynamic_slice(
            values, (place, 0, 0), (1, PAD, D), allow_negative_indices=False
        )[0]

    one = ring_scatter(
        lambda place: cut((0, place, 0, 0, 0), (4, 1, 1, PAD, D)).reshape(4, PAD, D), "x"
    )
    two = ring_scatter(
        lambda place: cut((place, 0, 1, 0, 0), (1, 4, 1, PAD, D)).reshape(4, PAD, D), "y"
    )
    one, two = ring_scatter(part_of(one), "y"), ring_scatter(part_of(two), "x")
    attn_part = depth_sum(jnp.stack([one, two]), zh)
    parts = lax.all_gather(early, ("y", "x"), axis=0, tiled=True).reshape(16, 2, PAD, D)
    grad_down = unpack(parts[:, 0], D)
    grad_up = unpack(parts[:, 1], QUART)
    attn_part = after(attn_part, parts)
    one, two = ring_gather(attn_part[:40], "x"), ring_gather(attn_part[40:], "y")
    one, two = ring_gather(one, "y"), ring_gather(two, "x")
    attn = jnp.concatenate([one, two.transpose(1, 0, 2, 3)], axis=2).reshape(16, PAD, D)
    attn = after(after(attn, grad_up), grad_down)
    grad_qkv = unpack(attn[:12], QUART)
    grad_out = unpack(attn[12:], QUART)
    vectors = attn[:12, SLICE, :VECTOR].reshape(-1).astype(F32)

    def owned(start, size):
        return vectors[start : start + size]

    return (
        block_output[None],
        grad_input[None],
        owned(0, QUART),
        owned(QUART, QUART),
        grad_qkv,
        owned(2 * QUART, QUART),
        owned(3 * QUART, QUART),
        grad_out,
        owned(4 * QUART, QUART),
        owned(5 * QUART, QUART),
        owned(6 * QUART, QUART),
        grad_up,
        owned(8 * QUART, D),
        grad_down,
        owned(7 * QUART, QUART),
    )


def solution(mesh):
    grid = Mesh(mesh.devices.reshape(4, 4, 2, 2, 2), AXES)
    rep, grp = ("y", "x", "zl"), ("zh", "c")
    tokens = P(rep, grp, None)
    vector, matrix = P(grp), P(grp, None)
    params = (
        vector,
        vector,
        matrix,
        vector,
        vector,
        matrix,
        vector,
        vector,
        vector,
        matrix,
        vector,
        matrix,
        vector,
    )
    return jax.shard_map(
        body,
        mesh=grid,
        in_specs=(tokens, P(rep, None)) + params + (tokens,),
        out_specs=(tokens, tokens) + params,
        check_vma=False,
    )
```

```python
import functools

import jax
import jax.numpy as jnp
from jax import lax
from jax.experimental import pallas as pl
from jax.experimental.layout import Layout, with_layout_constraint
from jax.experimental.pallas import tpu as pltpu
from jax.sharding import Mesh
from jax.sharding import PartitionSpec as P

D = 1088
HEADS = 17
HEAD = 64
QUART = 272
SLICE = 68
PAD = 72
VECTOR = 272
AXES = ("y", "x", "zl", "zh", "c")
BF = jnp.bfloat16
F32 = jnp.float32


def layer_norm(values, gain, shift):
    centre = values - jnp.mean(values, axis=-1, keepdims=True)
    spread = jnp.mean(centre * centre, axis=-1, keepdims=True)
    return centre * lax.rsqrt(spread + 1e-05) * gain + shift


def gelu_both(values):
    below = 0.5 * (1.0 + lax.erf(values * 0.7071067811865476))
    density = jnp.exp(values * values * -0.5) * 0.3989422804014327
    return values * below, below + values * density


def rows_major(x):
    return with_layout_constraint(x, Layout(major_to_minor=tuple(range(x.ndim))))


def permute(x, axis, pairs):
    shape = x.shape
    if shape[-2] % 128 == 0 and shape[-1] % 128 != 0:
        x = x.reshape(-1, 64, shape[-1])
    return rows_major(lax.ppermute(rows_major(x), axis, pairs)).reshape(shape)


def rotate(x, axis, step):
    return permute(x, axis, [(at, (at + step) % 4) for at in range(4)])


def swap_core(x):
    return permute(x, "c", [(0, 1), (1, 0)])


def swap_half(x):
    return permute(x, "zh", [(0, 1), (1, 0)])


def swap_near(x):
    return permute(x, "zl", [(0, 1), (1, 0)])


def swap_far(x):
    return permute(x, ("zl", "zh"), [(0, 3), (3, 0), (1, 2), (2, 1)])


def swap_pair(x, axis):
    return permute(x, axis, [(0, 1), (1, 0), (2, 3), (3, 2)])


def after_kernel(x_ref, done_ref, out_ref):
    pass


def after(x, done):
    if done.size > 2**19:
        done = done.reshape((-1,) + done.shape[-2:])[0, :8, :128]
    return pl.pallas_call(
        after_kernel,
        out_shape=jax.ShapeDtypeStruct(x.shape, x.dtype),
        in_specs=[pl.BlockSpec(memory_space=pl.ANY)] * 2,
        out_specs=pl.BlockSpec(memory_space=pl.ANY),
        input_output_aliases={0: 0},
    )(x, done)


def rows_of(values, start, size):
    return lax.dynamic_slice(
        values, (start, 0), (size, values.shape[1]), allow_negative_indices=False
    )


def natural(parts, place):
    found = []
    for index in range(4):
        value = parts[index]
        for at in range(1, 4):
            value = jnp.where(place == at, parts[(index - at) % 4], value)
        found.append(value)
    return jnp.stack(found)


def ring_scatter(part, axis):
    place = lax.axis_index(axis)
    got = [rotate(part((place + step) & 3), axis, step) for step in (2, 1, 3)]
    total = part(place).astype(F32)
    for value in got:
        total = total + value.astype(F32)
    return total.astype(BF)


def ring_scatter_halves(part, axis):
    place = lax.axis_index(axis)
    far, ahead, behind = (part((place + step) & 3) for step in (2, 1, 3))
    half = far.shape[0] // 2
    from_behind, from_ahead = rotate(far[:half], axis, 1), rotate(far[half:], axis, -1)

    def added(value, more):
        return (value.astype(F32) + more.astype(F32)).astype(BF)

    ahead = jnp.concatenate([added(ahead[:half], from_behind), ahead[half:]])
    behind = jnp.concatenate([behind[:half], added(behind[half:], from_ahead)])
    one, two = rotate(ahead, axis, 1), rotate(behind, axis, -1)
    total = part(place).astype(F32) + one.astype(F32) + two.astype(F32)
    return total.astype(BF)


def ring_gather(piece, axis):
    far, behind, ahead = (rotate(piece, axis, step) for step in (2, 1, 3))
    return natural([piece, ahead, far, behind], lax.axis_index(axis))


def depth_sum(values, zh, done=None):
    mine = jnp.where(zh == 0, values[0], values[1])
    other = jnp.where(zh == 0, values[1], values[0])
    far, half, near = swap_far(other), swap_half(other), swap_near(mine)
    if done is not None:
        near = after(near, done)
    total = mine.astype(F32) + near.astype(F32) + far.astype(F32) + half.astype(F32)
    return total.astype(BF)


def assemble_kernel(spots, *refs):
    *parts, out, sems = refs
    rows = out.shape[0] // 4
    rank = lax.axis_index("zh") * 2 + lax.axis_index("c")
    quarter = lax.axis_index("y") % 2 * 2 + lax.axis_index("x") % 2
    copies = []
    for which, row, flip, start, turn, size in spots:
        at = jnp.bitwise_xor(rank, flip) * rows + start
        if turn is not None:
            at = at + jnp.bitwise_xor(quarter, turn) * size
        copy = pltpu.make_async_copy(
            parts[which].at[pl.ds(row, size)],
            out.at[pl.ds(pl.multiple_of(at, 16), size)],
            sems.at[len(copies)],
        )
        copy.start()
        copies.append(copy)
    for copy in copies:
        copy.wait()


def assemble(rows, parts, spots):
    columns = parts[0].shape[1]
    return pl.pallas_call(
        functools.partial(assemble_kernel, spots),
        out_shape=jax.ShapeDtypeStruct((rows * 4, columns), BF),
        in_specs=[pl.BlockSpec(memory_space=pltpu.VMEM)] * len(parts),
        out_specs=pl.BlockSpec(memory_space=pl.ANY),
        scratch_shapes=[pltpu.SemaphoreType.DMA((len(spots),))],
        compiler_params=pltpu.CompilerParams(vmem_limit_bytes=24 * 2**20),
        cost_estimate=pl.CostEstimate(
            flops=0, bytes_accessed=rows * columns * 16, transcendentals=0
        ),
    )(*parts)


def dot_nt(left, right):
    return lax.dot_general(left, right, (((1,), (1,)), ((), ())), preferred_element_type=F32)


def dot_tn(left, right):
    return lax.dot_general(left, right, (((0,), (0,)), ((), ())), preferred_element_type=F32)


def attend_forward_kernel(q_ref, k_ref, v_ref, mask_ref, mixed_ref, total_ref):
    mask = mask_ref[...]
    queries, keys, values = q_ref[...], k_ref[...], v_ref[...]
    mixed, totals = [], []
    for head in range(2):
        lanes = slice(head * HEAD, (head + 1) * HEAD)
        scores = dot_nt(queries[:, lanes], keys[:, lanes]) * 0.125 + mask
        highest = jnp.max(scores, axis=1, keepdims=True)
        powers = jnp.exp(scores - highest)
        total = jnp.sum(powers, axis=1, keepdims=True)
        probs = (powers * (1.0 / total)).astype(BF)
        value = jnp.dot(probs, values[:, lanes], preferred_element_type=F32)
        mixed.append(value)
        totals.append(jnp.broadcast_to(highest + jnp.log(total), value.shape))
    mixed_ref[...] = jnp.concatenate(mixed, axis=1).astype(BF)
    total_ref[...] = jnp.concatenate(totals, axis=1)


def attend_backward_kernel(
    q_ref, k_ref, v_ref, mask_ref, total_ref, d_mixed_ref, dq_ref, keep_ref, send_ref
):
    mask = mask_ref[...]
    queries, keys, values = q_ref[...], k_ref[...], v_ref[...]
    totals, d_mixed = total_ref[...], d_mixed_ref[...]
    d_query, d_key, d_value = [], [], []
    for head in range(2):
        lanes = slice(head * HEAD, (head + 1) * HEAD)
        query, key, upstream = queries[:, lanes], keys[:, lanes], d_mixed[:, lanes]
        scores = dot_nt(query, key) * 0.125 + mask
        probs = jnp.exp(scores - totals[:, lanes][:, :1])
        weighted = probs * dot_nt(upstream, values[:, lanes])
        centred = jnp.sum(weighted, axis=1, keepdims=True)
        d_scores = (weighted - probs * centred).astype(BF)
        d_query.append(jnp.dot(d_scores, key, preferred_element_type=F32) * 0.125)
        d_key.append(dot_tn(d_scores, query) * 0.125)
        d_value.append(dot_tn(probs.astype(BF), upstream))
    dq_ref[...] = jnp.concatenate(d_query, axis=1).astype(BF)
    rows = dq_ref.shape[0]
    for at, parts in enumerate((d_key, d_value)):
        whole = jnp.concatenate(parts, axis=1).astype(BF)
        keep_ref[0, at] = whole[:rows]
        send_ref[0, at] = whole[rows : 2 * rows]
        keep_ref[1, at] = whole[2 * rows : 3 * rows]
        send_ref[1, at] = whole[3 * rows :]


def pair_spec(rows):
    return pl.BlockSpec((rows, 2 * HEAD), lambda at: (0, at))


def attend_forward(queries, keys, values, mask):
    rows, length = mask.shape
    return pl.pallas_call(
        attend_forward_kernel,
        grid=((HEADS + 1) // 2,),
        out_shape=(
            jax.ShapeDtypeStruct((rows, D), BF),
            jax.ShapeDtypeStruct((rows, D), F32),
        ),
        in_specs=[
            pair_spec(rows),
            pair_spec(length),
            pair_spec(length),
            pl.BlockSpec(mask.shape, lambda at: (0, 0)),
        ],
        out_specs=(pair_spec(rows), pair_spec(rows)),
        compiler_params=pltpu.CompilerParams(vmem_limit_bytes=32 * 2**20),
        cost_estimate=pl.CostEstimate(
            flops=4 * rows * length * D,
            bytes_accessed=24 * rows * D,
            transcendentals=HEADS * rows * length,
        ),
    )(queries, keys, values, mask)


def attend_backward(queries, keys, values, mask, totals, d_mixed):
    rows, length = mask.shape
    both = jax.ShapeDtypeStruct((2, 2, rows, D), BF)
    both_spec = pl.BlockSpec((2, 2, rows, 2 * HEAD), lambda at: (0, 0, 0, at))
    return pl.pallas_call(
        attend_backward_kernel,
        grid=((HEADS + 1) // 2,),
        out_shape=(jax.ShapeDtypeStruct((rows, D), BF), both, both),
        in_specs=[
            pair_spec(rows),
            pair_spec(length),
            pair_spec(length),
            pl.BlockSpec(mask.shape, lambda at: (0, 0)),
            pair_spec(rows),
            pair_spec(rows),
        ],
        out_specs=(pair_spec(rows), both_spec, both_spec),
        compiler_params=pltpu.CompilerParams(vmem_limit_bytes=32 * 2**20),
        cost_estimate=pl.CostEstimate(
            flops=10 * rows * length * D,
            bytes_accessed=48 * rows * D,
            transcendentals=HEADS * rows * length,
        ),
    )(queries, keys, values, mask, totals, d_mixed)


def weight_grad_kernel(count, first, *refs):
    lefts, rights = refs[:2], refs[2 : 2 + 2 * count]
    vector_ref, out_ref = refs[2 + 2 * count], refs[-1]
    left, left_other = lefts[0][0], lefts[1][0]
    pieces = left.shape[1] // SLICE
    done = 0
    for own, other in zip(rights[::2], rights[1::2]):
        for at in range(own.shape[-1] // D):
            lanes = slice(at * D, (at + 1) * D)
            product = dot_tn(left, own[:, lanes]) + dot_tn(left_other, other[:, lanes])
            for piece in range(pieces):
                part = product[piece * SLICE : (piece + 1) * SLICE]
                empty = jnp.zeros((PAD - SLICE, D), F32)
                if first == 0 and count == 3:
                    row = vector_ref[0, done : done + 1]
                    empty = jnp.concatenate([row, empty[1:]])
                out_ref[done, 0, 0] = jnp.concatenate([part, empty]).astype(BF)
                done += 1


def weight_grad(lefts, rights, vectors, slots, first, slot, buffer=None):
    _, tokens, width = lefts[0].shape
    rights = [value for pair in rights for value in pair]
    blocks = sum(value.shape[1] for value in rights[::2]) // D
    pieces = blocks * (width // SLICE)
    in_specs = [pl.BlockSpec((1, tokens, width), lambda at: (at, 0, 0))] * 2
    in_specs += [pl.BlockSpec(value.shape, lambda at: (0, 0)) for value in rights]
    in_specs += [pl.BlockSpec((1,) + vectors.shape[1:], lambda at: (at, 0, 0))]
    more = () if buffer is None else (buffer,)
    operands = (*lefts, *rights, vectors)
    return pl.pallas_call(
        functools.partial(weight_grad_kernel, len(rights) // 2, first),
        grid=(2,),
        out_shape=jax.ShapeDtypeStruct((16, slots, 2, PAD, D), BF),
        in_specs=in_specs + [pl.BlockSpec(memory_space=pl.ANY)] * len(more),
        out_specs=pl.BlockSpec(
            (pieces, 1, 1, PAD, D), lambda at: (first // pieces, slot, at, 0, 0)
        ),
        input_output_aliases={len(operands): 0} if more else {},
        compiler_params=pltpu.CompilerParams(vmem_limit_bytes=48 * 2**20),
        cost_estimate=pl.CostEstimate(
            flops=8 * tokens * width * blocks * D,
            bytes_accessed=2 * sum(value.size for value in operands) + 4 * pieces * PAD * D,
            transcendentals=0,
        ),
    )(*operands, *more)


def unpack_kernel(in_ref, out_ref):
    count, across = out_ref.shape[0] // SLICE, out_ref.shape[1] // D
    for at in range(across):
        for piece in range(count):
            part = in_ref[at * count + piece].astype(F32)[:SLICE]
            out_ref[piece * SLICE : (piece + 1) * SLICE, at * D : (at + 1) * D] = part


def unpack(pieces, rows):
    columns = pieces.shape[0] * SLICE // rows * D
    return pl.pallas_call(
        unpack_kernel,
        out_shape=jax.ShapeDtypeStruct((rows, columns), F32),
        in_specs=[pl.BlockSpec(memory_space=pltpu.VMEM)],
        out_specs=pl.BlockSpec(memory_space=pltpu.VMEM),
        compiler_params=pltpu.CompilerParams(vmem_limit_bytes=24 * 2**20),
        cost_estimate=pl.CostEstimate(
            flops=0, bytes_accessed=pieces.size * 6, transcendentals=0
        ),
    )(pieces)


def gather_quarters(shard):
    across, down = lax.axis_index("x") & 1, lax.axis_index("y") & 1
    piece = rows_of(shard, (down * 2 + across) * 64, 64)
    got = swap_far(jnp.concatenate([piece, shard[256:]]))
    mine = got[:64]
    by_x, by_y = swap_pair(mine, "x"), swap_pair(mine, "y")
    last = swap_pair(by_y, "x")
    return by_x, jnp.concatenate([got, by_x, by_y, last])


def widened(value):
    size = value.shape[0] // 4
    return jnp.concatenate([value[at * size : (at + 1) * size] for at in range(4)], axis=1)


def narrowed(value):
    return jnp.stack([value[:, :, at * D : (at + 1) * D] for at in range(4)], axis=1).reshape(-1, D)


def start_mlp(w_up, w_down, small, spot, done):
    sent = [
        rows_of(w_up, spot * 16, 16),
        widened(rows_of(w_down, spot * 64, 64)),
        w_up[256:],
        widened(w_down[1024:]),
        small,
    ]
    got = swap_far(after(jnp.concatenate(sent), done))
    rest = got[32:]
    across_rest = swap_core(jnp.concatenate([rest, small]))
    far = lax.all_gather(got[:32], ("y", "x"), axis=0, tiled=True)
    smalls = [small[0], across_rest[48], rest[32], across_rest[32]]
    return got, far, across_rest, [value[: 12 * QUART].astype(F32) for value in smalls]


def finish_mlp(w_up, w_down, got, far, across_rest):
    rest = got[32:]
    across = swap_core(far).reshape(16, 32, 4 * D)
    far = far.reshape(16, 32, 4 * D)
    up = assemble(
        QUART,
        (
            w_up,
            swap_core(w_up),
            far[:, :16].reshape(256, 4 * D),
            rest,
            across[:, :16].reshape(256, 4 * D),
            across_rest,
        ),
        (
            (0, 0, 0, 0, None, QUART),
            (1, 0, 1, 0, None, QUART),
            (2, 0, 2, 0, None, 256),
            (3, 0, 2, 256, None, 16),
            (4, 0, 3, 0, None, 256),
            (5, 0, 3, 256, None, 16),
        ),
    )
    down = assemble(
        D,
        (
            w_down,
            swap_core(w_down),
            narrowed(far[:, 16:]),
            narrowed(rest[None, 16:32]),
            narrowed(across[:, 16:]),
            narrowed(across_rest[None, 16:32]),
        ),
        (
            (0, 0, 0, 0, None, D),
            (1, 0, 1, 0, None, D),
            (2, 0, 2, 0, None, 1024),
            (3, 0, 2, 1024, None, 64),
            (4, 0, 3, 0, None, 1024),
            (5, 0, 3, 1024, None, 64),
        ),
    )
    return up, down


def body(
    block_input,
    segment_ids,
    attn_gain,
    attn_shift,
    w_qkv,
    bias_query,
    bias_value,
    w_out,
    bias_out,
    mlp_gain,
    mlp_shift,
    w_up,
    bias_up,
    w_down,
    bias_down,
    cotangent,
):
    core, zh = lax.axis_index("c"), lax.axis_index("zh")
    rank = zh * 2 + core
    spot = lax.axis_index("y") * 4 + lax.axis_index("x")
    small = jnp.concatenate(
        [
            attn_gain,
            attn_shift,
            bias_query,
            bias_value,
            bias_out,
            mlp_gain,
            mlp_shift,
            bias_up,
            bias_down,
        ]
    )
    small = jnp.pad(small[None], ((0, 15), (0, D)))
    rows = block_input.shape[1]
    own_tokens = block_input[0]
    by_x, far_parts = gather_quarters(w_qkv)
    across_parts = swap_core(far_parts)
    half_tokens = swap_half(after(own_tokens, by_x))
    tokens = [own_tokens, swap_core(own_tokens), half_tokens, swap_core(half_tokens)]
    got_mlp, far_mlp, across_rest, smalls = start_mlp(w_up, w_down, small, spot, across_parts)
    turns = ((0, 0, 0, 64), (80, 0, 1, 64), (144, 0, 2, 64), (208, 0, 3, 64), (64, 256, None, 16))
    full_qkv = assemble(
        QUART,
        (w_qkv, swap_core(w_qkv), far_parts, across_parts),
        ((0, 0, 0, 0, None, QUART), (1, 0, 1, 0, None, QUART))
        + tuple((2, row, 2, *turn) for row, *turn in turns)
        + tuple((3, row, 3, *turn) for row, *turn in turns),
    )
    far_out = after(swap_far(after(w_out, got_mlp)), full_qkv)
    full_out = assemble(
        QUART,
        (w_out, swap_core(w_out), far_out, swap_core(far_out)),
        tuple((flip, 0, flip, 0, None, QUART) for flip in range(4)),
    )

    ordered = []
    for index in range(4):
        value = smalls[index]
        for at in range(1, 4):
            value = jnp.where(rank == at, smalls[index ^ at], value)
        ordered.append(value)
    ordered = jnp.stack(ordered)

    def vector(start, size):
        return ordered[:, start : start + size].reshape(-1)

    gain_one, shift_one, query_bias, value_bias, out_bias, gain_two, shift_two = (
        vector(QUART * index, QUART) for index in range(7)
    )
    up_bias = vector(7 * QUART, D)
    down_bias = vector(11 * QUART, QUART)

    segments = segment_ids[0]
    upstream = cotangent[0]

    hidden_in = own_tokens.astype(F32)
    normed_parts = [
        layer_norm(part.astype(F32), gain_one, shift_one).astype(BF) for part in tokens
    ]
    normed = normed_parts[0]
    normed_all = jnp.concatenate(normed_parts)
    queries = (
        jnp.dot(normed, full_qkv[:, :D], preferred_element_type=F32) + query_bias
    ).astype(BF)
    keys = jnp.dot(normed_all, full_qkv[:, D : 2 * D], preferred_element_type=F32).astype(BF)
    values = jnp.dot(normed_all, full_qkv[:, 2 * D :], preferred_element_type=F32)
    values = (values + value_bias).astype(BF)
    query_places = rank * rows + jnp.arange(rows)
    starts = [jnp.bitwise_xor(rank, flip) * rows for flip in range(4)]
    key_places = jnp.concatenate([start + jnp.arange(rows) for start in starts])
    key_segments = jnp.concatenate(
        [
            lax.dynamic_slice(segments, (start,), (rows,), allow_negative_indices=False)
            for start in starts
        ]
    )
    allowed = (key_segments[:rows, None] == key_segments[None, :]) & (
        query_places[:, None] >= key_places[None, :]
    )
    mask = jnp.where(allowed, 0.0, -1e30).astype(F32)
    mixed, log_total = attend_forward(queries, keys, values, mask)
    far_mlp = after(far_mlp, mixed)
    full_up, full_down = finish_mlp(w_up, w_down, got_mlp, far_mlp, across_rest)
    middle = hidden_in + jnp.dot(mixed, full_out, preferred_element_type=F32) + out_bias
    normed_two = layer_norm(middle, gain_two, shift_two).astype(BF)
    upper = jnp.dot(normed_two, full_up, preferred_element_type=F32) + up_bias
    activated, slope = gelu_both(upper)
    activated = activated.astype(BF)
    block_output = middle + jnp.dot(activated, full_down, preferred_element_type=F32) + down_bias

    def paired(value):
        return value, swap_core(value)

    def paired_columns(value):
        width = value.shape[1] // 4
        blocks = [value[:, at * width : (at + 1) * width] for at in range(4)]
        even, odd = jnp.stack([blocks[0], blocks[2]]), jnp.stack([blocks[1], blocks[3]])
        mine = jnp.where(core == 0, even, odd)
        other = jnp.where(core == 0, odd, even)
        return mine, swap_core(other)

    upstream_wide = upstream.astype(F32)
    upstream_pair = paired(upstream)
    grad_down_bias = jnp.sum(upstream_wide, axis=0)
    activated_pair = paired_columns(activated)

    d_activated = jnp.dot(upstream, full_down.T, preferred_element_type=F32)
    d_upper = (d_activated * slope).astype(BF)
    grad_up_bias = jnp.sum(d_upper.astype(F32), axis=0)
    normed_two_pair, d_upper_pair = paired_columns(normed_two), paired(d_upper)
    no_vectors = jnp.zeros((2, 12, D), F32)
    grad_mlp = weight_grad(activated_pair, [upstream_pair], no_vectors, 2, 0, 0)
    grad_mlp = weight_grad(
        normed_two_pair, [d_upper_pair], no_vectors, 2, 0, 1, grad_mlp
    )
    mlp_part = lax.psum_scatter(
        grad_mlp.reshape(64 * PAD, D), ("y", "x"), scatter_dimension=0, tiled=True
    ).reshape(2, 2, PAD, D)

    d_normed_two = jnp.dot(d_upper, full_up.T, preferred_element_type=F32)
    norm_two_back = jax.vjp(layer_norm, middle, gain_two, shift_two)[1]
    d_middle_part, grad_gain_two, grad_shift_two = norm_two_back(d_normed_two)
    d_middle = upstream_wide + d_middle_part
    d_attended = d_middle.astype(BF)
    grad_out_bias = jnp.sum(d_attended.astype(F32), axis=0)
    mixed_pair, d_attended_pair = paired_columns(mixed), paired(d_attended)
    normed_pair = paired_columns(normed)

    d_mixed = jnp.dot(d_attended, full_out.T, preferred_element_type=F32).astype(BF)
    d_queries, d_both, d_beside = attend_backward(
        queries, keys, values, mask, log_total, after(d_mixed, grad_mlp)
    )
    d_beside = swap_core(d_beside)
    d_half = swap_half((d_both[1].astype(F32) + d_beside[1].astype(F32)).astype(BF))
    queries_pair = paired(d_queries)
    grad_attn = weight_grad(mixed_pair, [d_attended_pair], no_vectors, 1, 12, 0)
    d_half = after(after(after(d_half, grad_attn), queries_pair[1]), normed_pair[1])
    d_both = d_both[0].astype(F32) + d_beside[0].astype(F32) + d_half.astype(F32)
    d_both = d_both.astype(BF)
    d_keys, d_values = d_both[0], d_both[1]
    grad_query_bias = jnp.sum(d_queries.astype(F32), axis=0)
    grad_value_bias = jnp.sum(d_values.astype(F32), axis=0)
    rights = [queries_pair, paired(d_keys), paired(d_values)]
    d_normed = None
    for at, part in enumerate((d_queries, d_keys, d_values)):
        term = lax.dot_general(
            part,
            full_qkv[:, at * D : (at + 1) * D],
            (((1,), (1,)), ((), ())),
            preferred_element_type=F32,
        )
        d_normed = term if d_normed is None else d_normed + term
    norm_one_back = jax.vjp(layer_norm, hidden_in, gain_one, shift_one)[1]
    d_input_part, grad_gain_one, grad_shift_one = norm_one_back(d_normed)
    grad_input = d_middle + d_input_part

    vectors = jnp.concatenate(
        [
            value.reshape(4, -1)
            for value in (
                grad_gain_one,
                grad_shift_one,
                grad_query_bias,
                grad_value_bias,
                grad_out_bias,
                grad_gain_two,
                grad_shift_two,
                grad_down_bias,
                grad_up_bias,
            )
        ],
        axis=1,
    )
    even, odd = vectors[0::2], vectors[1::2]
    mine = jnp.where(core == 0, even, odd)
    other = jnp.where(core == 0, odd, even)
    mine = (mine + swap_core(other.astype(BF)).astype(F32)).astype(BF)
    mine = jnp.pad(mine.reshape(2, 12, VECTOR).astype(F32), ((0, 0), (0, 0), (0, D - VECTOR)))

    grad_attn = weight_grad(normed_pair, rights, mine, 1, 0, 0, grad_attn)
    early = depth_sum(mlp_part.transpose(1, 0, 2, 3).reshape(2, 2 * PAD, D), zh, grad_attn)
    grad_attn = grad_attn.reshape(4, 4, 2, PAD, D)

    def cut(start, size):
        return lax.dynamic_slice(grad_attn, start, size, allow_negative_indices=False)

    def part_of(values):
        return lambda place: cut_row(values, place)

    def cut_row(values, place):
        return lax.dynamic_slice(
            values, (place, 0, 0), (1, PAD, D), allow_negative_indices=False
        )[0]

    one = ring_scatter_halves(
        lambda place: cut((0, place, 0, 0, 0), (4, 1, 1, PAD, D)).reshape(4, PAD, D), "x"
    )
    two = ring_scatter_halves(
        lambda place: cut((place, 0, 1, 0, 0), (1, 4, 1, PAD, D)).reshape(4, PAD, D), "y"
    )
    one, two = ring_scatter(part_of(one), "y"), ring_scatter(part_of(two), "x")
    attn_part = depth_sum(jnp.stack([one, two]), zh)
    parts = lax.all_gather(early, ("y", "x"), axis=0, tiled=True).reshape(16, 2, PAD, D)
    grad_down = unpack(parts[:, 0], D)
    grad_up = unpack(parts[:, 1], QUART)
    attn_part = after(attn_part, parts)
    one, two = ring_gather(attn_part[:40], "x"), ring_gather(attn_part[40:], "y")
    one, two = ring_gather(one, "y"), ring_gather(two, "x")
    attn = jnp.concatenate([one, two.transpose(1, 0, 2, 3)], axis=2).reshape(16, PAD, D)
    attn = after(after(attn, grad_up), grad_down)
    grad_qkv = unpack(attn[:12], QUART)
    grad_out = unpack(attn[12:], QUART)
    vectors = attn[:12, SLICE, :VECTOR].reshape(-1).astype(F32)

    def owned(start, size):
        return vectors[start : start + size]

    return (
        block_output[None],
        grad_input[None],
        owned(0, QUART),
        owned(QUART, QUART),
        grad_qkv,
        owned(2 * QUART, QUART),
        owned(3 * QUART, QUART),
        grad_out,
        owned(4 * QUART, QUART),
        owned(5 * QUART, QUART),
        owned(6 * QUART, QUART),
        grad_up,
        owned(8 * QUART, D),
        grad_down,
        owned(7 * QUART, QUART),
    )


def solution(mesh):
    grid = Mesh(mesh.devices.reshape(4, 4, 2, 2, 2), AXES)
    rep, grp = ("y", "x", "zl"), ("zh", "c")
    tokens = P(rep, grp, None)
    vector, matrix = P(grp), P(grp, None)
    params = (
        vector,
        vector,
        matrix,
        vector,
        vector,
        matrix,
        vector,
        vector,
        vector,
        matrix,
        vector,
        matrix,
        vector,
    )
    return jax.shard_map(
        body,
        mesh=grid,
        in_specs=(tokens, P(rep, None)) + params + (tokens,),
        out_specs=(tokens, tokens) + params,
        check_vma=False,
    )
```

```python
import functools

import jax
import jax.numpy as jnp
from jax import lax
from jax.experimental import pallas as pl
from jax.experimental.layout import Layout, with_layout_constraint
from jax.experimental.pallas import tpu as pltpu
from jax.sharding import Mesh
from jax.sharding import PartitionSpec as P

D = 1088
HEADS = 17
HEAD = 64
QUART = 272
SLICE = 68
PAD = 72
VECTOR = 272
AXES = ("y", "x", "zl", "zh", "c")
BF = jnp.bfloat16
F32 = jnp.float32


def layer_norm(values, gain, shift):
    centre = values - jnp.mean(values, axis=-1, keepdims=True)
    spread = jnp.mean(centre * centre, axis=-1, keepdims=True)
    return centre * lax.rsqrt(spread + 1e-05) * gain + shift


def gelu_both(values):
    below = 0.5 * (1.0 + lax.erf(values * 0.7071067811865476))
    density = jnp.exp(values * values * -0.5) * 0.3989422804014327
    return values * below, below + values * density


def rows_major(x):
    return with_layout_constraint(x, Layout(major_to_minor=tuple(range(x.ndim))))


def permute(x, axis, pairs):
    shape = x.shape
    if shape[-2] % 128 == 0 and shape[-1] % 128 != 0:
        x = x.reshape(-1, 64, shape[-1])
    return rows_major(lax.ppermute(rows_major(x), axis, pairs)).reshape(shape)


def rotate(x, axis, step):
    return permute(x, axis, [(at, (at + step) % 4) for at in range(4)])


def swap_core(x):
    return permute(x, "c", [(0, 1), (1, 0)])


def swap_half(x):
    return permute(x, "zh", [(0, 1), (1, 0)])


def swap_near(x):
    return permute(x, "zl", [(0, 1), (1, 0)])


def swap_far(x):
    return permute(x, ("zl", "zh"), [(0, 3), (3, 0), (1, 2), (2, 1)])


def swap_pair(x, axis):
    return permute(x, axis, [(0, 1), (1, 0), (2, 3), (3, 2)])


def after_kernel(x_ref, done_ref, out_ref):
    pass


def after(x, done):
    if done.size > 2**19:
        done = done.reshape((-1,) + done.shape[-2:])[0, :8, :128]
    return pl.pallas_call(
        after_kernel,
        out_shape=jax.ShapeDtypeStruct(x.shape, x.dtype),
        in_specs=[pl.BlockSpec(memory_space=pl.ANY)] * 2,
        out_specs=pl.BlockSpec(memory_space=pl.ANY),
        input_output_aliases={0: 0},
    )(x, done)


def rows_of(values, start, size):
    return lax.dynamic_slice(
        values, (start, 0), (size, values.shape[1]), allow_negative_indices=False
    )


def natural(parts, place):
    found = []
    for index in range(4):
        value = parts[index]
        for at in range(1, 4):
            value = jnp.where(place == at, parts[(index - at) % 4], value)
        found.append(value)
    return jnp.stack(found)


def ring_scatter(part, axis):
    place = lax.axis_index(axis)
    got = [rotate(part((place + step) & 3), axis, step) for step in (2, 1, 3)]
    total = part(place).astype(F32)
    for value in got:
        total = total + value.astype(F32)
    return total.astype(BF)


def ring_scatter_halves(part, axis):
    place = lax.axis_index(axis)
    far, ahead, behind = (part((place + step) & 3) for step in (2, 1, 3))
    half = far.shape[0] // 2
    from_behind, from_ahead = rotate(far[:half], axis, 1), rotate(far[half:], axis, -1)

    def added(value, more):
        return (value.astype(F32) + more.astype(F32)).astype(BF)

    ahead = jnp.concatenate([added(ahead[:half], from_behind), ahead[half:]])
    behind = jnp.concatenate([behind[:half], added(behind[half:], from_ahead)])
    one, two = rotate(ahead, axis, 1), rotate(behind, axis, -1)
    total = part(place).astype(F32) + one.astype(F32) + two.astype(F32)
    return total.astype(BF)


def ring_gather(piece, axis):
    far, behind, ahead = (rotate(piece, axis, step) for step in (2, 1, 3))
    return natural([piece, ahead, far, behind], lax.axis_index(axis))


def depth_sum(values, zh, done=None):
    mine = jnp.where(zh == 0, values[0], values[1])
    other = jnp.where(zh == 0, values[1], values[0])
    far, half, near = swap_far(other), swap_half(other), swap_near(mine)
    if done is not None:
        near = after(near, done)
    total = mine.astype(F32) + near.astype(F32) + far.astype(F32) + half.astype(F32)
    return total.astype(BF)


def assemble_kernel(spots, *refs):
    *parts, out, sems = refs
    rows = out.shape[0] // 4
    rank = lax.axis_index("zh") * 2 + lax.axis_index("c")
    quarter = lax.axis_index("y") % 2 * 2 + lax.axis_index("x") % 2
    copies = []
    for which, row, flip, start, turn, size in spots:
        at = jnp.bitwise_xor(rank, flip) * rows + start
        if turn is not None:
            at = at + jnp.bitwise_xor(quarter, turn) * size
        copy = pltpu.make_async_copy(
            parts[which].at[pl.ds(row, size)],
            out.at[pl.ds(pl.multiple_of(at, 16), size)],
            sems.at[len(copies)],
        )
        copy.start()
        copies.append(copy)
    for copy in copies:
        copy.wait()


def assemble(rows, parts, spots):
    columns = parts[0].shape[1]
    return pl.pallas_call(
        functools.partial(assemble_kernel, spots),
        out_shape=jax.ShapeDtypeStruct((rows * 4, columns), BF),
        in_specs=[pl.BlockSpec(memory_space=pltpu.VMEM)] * len(parts),
        out_specs=pl.BlockSpec(memory_space=pl.ANY),
        scratch_shapes=[pltpu.SemaphoreType.DMA((len(spots),))],
        compiler_params=pltpu.CompilerParams(vmem_limit_bytes=24 * 2**20),
        cost_estimate=pl.CostEstimate(
            flops=0, bytes_accessed=rows * columns * 16, transcendentals=0
        ),
    )(*parts)


def dot_nt(left, right):
    return lax.dot_general(left, right, (((1,), (1,)), ((), ())), preferred_element_type=F32)


def dot_tn(left, right):
    return lax.dot_general(left, right, (((0,), (0,)), ((), ())), preferred_element_type=F32)


def attend_forward_kernel(q_ref, k_ref, v_ref, mask_ref, mixed_ref, total_ref):
    mask = mask_ref[...]
    queries, keys, values = q_ref[...], k_ref[...], v_ref[...]
    mixed, totals = [], []
    for head in range(2):
        lanes = slice(head * HEAD, (head + 1) * HEAD)
        scores = dot_nt(queries[:, lanes], keys[:, lanes]) * 0.125 + mask
        highest = jnp.max(scores, axis=1, keepdims=True)
        powers = jnp.exp(scores - highest)
        total = jnp.sum(powers, axis=1, keepdims=True)
        probs = (powers * (1.0 / total)).astype(BF)
        value = jnp.dot(probs, values[:, lanes], preferred_element_type=F32)
        mixed.append(value)
        totals.append(jnp.broadcast_to(highest + jnp.log(total), value.shape))
    mixed_ref[...] = jnp.concatenate(mixed, axis=1).astype(BF)
    total_ref[...] = jnp.concatenate(totals, axis=1)


def attend_backward_kernel(
    q_ref, k_ref, v_ref, mask_ref, total_ref, d_mixed_ref, dq_ref, keep_ref, send_ref
):
    mask = mask_ref[...]
    queries, keys, values = q_ref[...], k_ref[...], v_ref[...]
    totals, d_mixed = total_ref[...], d_mixed_ref[...]
    d_query, d_key, d_value = [], [], []
    for head in range(2):
        lanes = slice(head * HEAD, (head + 1) * HEAD)
        query, key, upstream = queries[:, lanes], keys[:, lanes], d_mixed[:, lanes]
        scores = dot_nt(query, key) * 0.125 + mask
        probs = jnp.exp(scores - totals[:, lanes][:, :1])
        weighted = probs * dot_nt(upstream, values[:, lanes])
        centred = jnp.sum(weighted, axis=1, keepdims=True)
        d_scores = (weighted - probs * centred).astype(BF)
        d_query.append(jnp.dot(d_scores, key, preferred_element_type=F32) * 0.125)
        d_key.append(dot_tn(d_scores, query) * 0.125)
        d_value.append(dot_tn(probs.astype(BF), upstream))
    dq_ref[...] = jnp.concatenate(d_query, axis=1).astype(BF)
    rows = dq_ref.shape[0]
    for at, parts in enumerate((d_key, d_value)):
        whole = jnp.concatenate(parts, axis=1).astype(BF)
        keep_ref[0, at] = whole[:rows]
        send_ref[0, at] = whole[rows : 2 * rows]
        keep_ref[1, at] = whole[2 * rows : 3 * rows]
        send_ref[1, at] = whole[3 * rows :]


def pair_spec(rows):
    return pl.BlockSpec((rows, 2 * HEAD), lambda at: (0, at))


def attend_forward(queries, keys, values, mask):
    rows, length = mask.shape
    return pl.pallas_call(
        attend_forward_kernel,
        grid=((HEADS + 1) // 2,),
        out_shape=(
            jax.ShapeDtypeStruct((rows, D), BF),
            jax.ShapeDtypeStruct((rows, D), F32),
        ),
        in_specs=[
            pair_spec(rows),
            pair_spec(length),
            pair_spec(length),
            pl.BlockSpec(mask.shape, lambda at: (0, 0)),
        ],
        out_specs=(pair_spec(rows), pair_spec(rows)),
        compiler_params=pltpu.CompilerParams(vmem_limit_bytes=32 * 2**20),
        cost_estimate=pl.CostEstimate(
            flops=4 * rows * length * D,
            bytes_accessed=24 * rows * D,
            transcendentals=HEADS * rows * length,
        ),
    )(queries, keys, values, mask)


def attend_backward(queries, keys, values, mask, totals, d_mixed):
    rows, length = mask.shape
    both = jax.ShapeDtypeStruct((2, 2, rows, D), BF)
    both_spec = pl.BlockSpec((2, 2, rows, 2 * HEAD), lambda at: (0, 0, 0, at))
    return pl.pallas_call(
        attend_backward_kernel,
        grid=((HEADS + 1) // 2,),
        out_shape=(jax.ShapeDtypeStruct((rows, D), BF), both, both),
        in_specs=[
            pair_spec(rows),
            pair_spec(length),
            pair_spec(length),
            pl.BlockSpec(mask.shape, lambda at: (0, 0)),
            pair_spec(rows),
            pair_spec(rows),
        ],
        out_specs=(pair_spec(rows), both_spec, both_spec),
        compiler_params=pltpu.CompilerParams(vmem_limit_bytes=32 * 2**20),
        cost_estimate=pl.CostEstimate(
            flops=10 * rows * length * D,
            bytes_accessed=48 * rows * D,
            transcendentals=HEADS * rows * length,
        ),
    )(queries, keys, values, mask, totals, d_mixed)


def weight_grad_kernel(count, first, *refs):
    lefts, rights = refs[:2], refs[2 : 2 + 2 * count]
    vector_ref, out_ref = refs[2 + 2 * count], refs[-1]
    left, left_other = lefts[0][0], lefts[1][0]
    pieces = left.shape[1] // SLICE
    done = 0
    for own, other in zip(rights[::2], rights[1::2]):
        for at in range(own.shape[-1] // D):
            lanes = slice(at * D, (at + 1) * D)
            product = dot_tn(left, own[:, lanes]) + dot_tn(left_other, other[:, lanes])
            for piece in range(pieces):
                part = product[piece * SLICE : (piece + 1) * SLICE]
                empty = jnp.zeros((PAD - SLICE, D), F32)
                if first == 0 and count == 3:
                    row = vector_ref[0, done : done + 1]
                    empty = jnp.concatenate([row, empty[1:]])
                out_ref[done, 0, 0] = jnp.concatenate([part, empty]).astype(BF)
                done += 1


def weight_grad(lefts, rights, vectors, slots, first, slot, buffer=None):
    _, tokens, width = lefts[0].shape
    rights = [value for pair in rights for value in pair]
    blocks = sum(value.shape[1] for value in rights[::2]) // D
    pieces = blocks * (width // SLICE)
    in_specs = [pl.BlockSpec((1, tokens, width), lambda at: (at, 0, 0))] * 2
    in_specs += [pl.BlockSpec(value.shape, lambda at: (0, 0)) for value in rights]
    in_specs += [pl.BlockSpec((1,) + vectors.shape[1:], lambda at: (at, 0, 0))]
    more = () if buffer is None else (buffer,)
    operands = (*lefts, *rights, vectors)
    return pl.pallas_call(
        functools.partial(weight_grad_kernel, len(rights) // 2, first),
        grid=(2,),
        out_shape=jax.ShapeDtypeStruct((16, slots, 2, PAD, D), BF),
        in_specs=in_specs + [pl.BlockSpec(memory_space=pl.ANY)] * len(more),
        out_specs=pl.BlockSpec(
            (pieces, 1, 1, PAD, D), lambda at: (first // pieces, slot, at, 0, 0)
        ),
        input_output_aliases={len(operands): 0} if more else {},
        compiler_params=pltpu.CompilerParams(vmem_limit_bytes=48 * 2**20),
        cost_estimate=pl.CostEstimate(
            flops=8 * tokens * width * blocks * D,
            bytes_accessed=2 * sum(value.size for value in operands) + 4 * pieces * PAD * D,
            transcendentals=0,
        ),
    )(*operands, *more)


def unpack_kernel(in_ref, out_ref):
    count, across = out_ref.shape[0] // SLICE, out_ref.shape[1] // D
    for at in range(across):
        for piece in range(count):
            part = in_ref[at * count + piece].astype(F32)[:SLICE]
            out_ref[piece * SLICE : (piece + 1) * SLICE, at * D : (at + 1) * D] = part


def unpack(pieces, rows):
    columns = pieces.shape[0] * SLICE // rows * D
    return pl.pallas_call(
        unpack_kernel,
        out_shape=jax.ShapeDtypeStruct((rows, columns), F32),
        in_specs=[pl.BlockSpec(memory_space=pltpu.VMEM)],
        out_specs=pl.BlockSpec(memory_space=pltpu.VMEM),
        compiler_params=pltpu.CompilerParams(vmem_limit_bytes=24 * 2**20),
        cost_estimate=pl.CostEstimate(
            flops=0, bytes_accessed=pieces.size * 6, transcendentals=0
        ),
    )(pieces)


def unpack_pair_kernel(one_ref, two_ref, wide_ref, last_ref):
    for down in range(4):
        for across in range(4):
            one, two = one_ref[down, across].astype(F32), two_ref[across, down].astype(F32)
            part = jnp.concatenate([one, two[: SLICE - one.shape[0]]])
            lines = slice(across * SLICE, (across + 1) * SLICE)
            if down < 3:
                wide_ref[lines, down * D : (down + 1) * D] = part
            else:
                last_ref[lines, :] = part


def unpack_pair(one, two):
    return pl.pallas_call(
        unpack_pair_kernel,
        out_shape=(
            jax.ShapeDtypeStruct((QUART, 3 * D), F32),
            jax.ShapeDtypeStruct((QUART, D), F32),
        ),
        in_specs=[pl.BlockSpec(memory_space=pltpu.VMEM)] * 2,
        out_specs=(pl.BlockSpec(memory_space=pltpu.VMEM),) * 2,
        compiler_params=pltpu.CompilerParams(vmem_limit_bytes=24 * 2**20),
        cost_estimate=pl.CostEstimate(
            flops=0, bytes_accessed=(one.size + two.size) * 6, transcendentals=0
        ),
    )(one, two)


def gather_quarters(shard):
    across, down = lax.axis_index("x") & 1, lax.axis_index("y") & 1
    piece = rows_of(shard, (down * 2 + across) * 64, 64)
    got = swap_far(jnp.concatenate([piece, shard[256:]]))
    mine = got[:64]
    by_x, by_y = swap_pair(mine, "x"), swap_pair(mine, "y")
    last = swap_pair(by_y, "x")
    return jnp.concatenate([got, by_x, by_y, last])


def widened(value):
    size = value.shape[0] // 4
    return jnp.concatenate([value[at * size : (at + 1) * size] for at in range(4)], axis=1)


def narrowed(value):
    return jnp.stack([value[:, :, at * D : (at + 1) * D] for at in range(4)], axis=1).reshape(-1, D)


def start_mlp(w_up, w_down, spot, done, done_rest):
    sent = [rows_of(w_up, spot * 16, 16), widened(rows_of(w_down, spot * 64, 64))]
    got = swap_far(after(jnp.concatenate(sent), done))
    far = lax.all_gather(got, ("y", "x"), axis=0, tiled=True)
    rest = swap_far(after(jnp.concatenate([w_up[256:], widened(w_down[1024:])]), done_rest))
    return far, rest, swap_core(rest)


def finish_mlp(w_up, w_down, rest, far, across_rest):
    across = swap_core(far).reshape(16, 32, 4 * D)
    far = far.reshape(16, 32, 4 * D)
    up = assemble(
        QUART,
        (
            w_up,
            swap_core(w_up),
            far[:, :16].reshape(256, 4 * D),
            rest,
            across[:, :16].reshape(256, 4 * D),
            across_rest,
        ),
        (
            (0, 0, 0, 0, None, QUART),
            (1, 0, 1, 0, None, QUART),
            (2, 0, 2, 0, None, 256),
            (3, 0, 2, 256, None, 16),
            (4, 0, 3, 0, None, 256),
            (5, 0, 3, 256, None, 16),
        ),
    )
    down = assemble(
        D,
        (
            w_down,
            swap_core(w_down),
            narrowed(far[:, 16:]),
            narrowed(rest[None, 16:32]),
            narrowed(across[:, 16:]),
            narrowed(across_rest[None, 16:32]),
        ),
        (
            (0, 0, 0, 0, None, D),
            (1, 0, 1, 0, None, D),
            (2, 0, 2, 0, None, 1024),
            (3, 0, 2, 1024, None, 64),
            (4, 0, 3, 0, None, 1024),
            (5, 0, 3, 1024, None, 64),
        ),
    )
    return up, down


def body(
    block_input,
    segment_ids,
    attn_gain,
    attn_shift,
    w_qkv,
    bias_query,
    bias_value,
    w_out,
    bias_out,
    mlp_gain,
    mlp_shift,
    w_up,
    bias_up,
    w_down,
    bias_down,
    cotangent,
):
    core, zh = lax.axis_index("c"), lax.axis_index("zh")
    rank = zh * 2 + core
    spot = lax.axis_index("y") * 4 + lax.axis_index("x")
    small = jnp.concatenate(
        [
            attn_gain,
            attn_shift,
            bias_query,
            bias_value,
            bias_out,
            mlp_gain,
            mlp_shift,
            bias_up,
            bias_down,
        ]
    )
    small = jnp.pad(small.reshape(3, D), ((0, 13), (0, 0)))
    rows = block_input.shape[1]
    own_tokens = block_input[0]
    far_parts = gather_quarters(w_qkv)
    with_small = jnp.concatenate([own_tokens, small])
    half = swap_half(with_small)
    token_parts = [with_small, swap_core(with_small), half, swap_core(half)]
    tokens = [part[:rows] for part in token_parts]
    smalls = [part[rows : rows + 3].reshape(-1).astype(F32) for part in token_parts]
    across_parts = swap_core(far_parts)
    far_mlp, got_rest, across_rest = start_mlp(
        w_up, w_down, spot, far_parts, across_parts
    )
    turns = ((0, 0, 0, 64), (80, 0, 1, 64), (144, 0, 2, 64), (208, 0, 3, 64), (64, 256, None, 16))
    full_qkv = assemble(
        QUART,
        (w_qkv, swap_core(w_qkv), far_parts, across_parts),
        ((0, 0, 0, 0, None, QUART), (1, 0, 1, 0, None, QUART))
        + tuple((2, row, 2, *turn) for row, *turn in turns)
        + tuple((3, row, 3, *turn) for row, *turn in turns),
    )
    far_out = after(swap_far(after(w_out, got_rest)), full_qkv)
    full_out = assemble(
        QUART,
        (w_out, swap_core(w_out), far_out, swap_core(far_out)),
        tuple((flip, 0, flip, 0, None, QUART) for flip in range(4)),
    )

    ordered = []
    for index in range(4):
        value = smalls[index]
        for at in range(1, 4):
            value = jnp.where(rank == at, smalls[index ^ at], value)
        ordered.append(value)
    ordered = jnp.stack(ordered)

    def vector(start, size):
        return ordered[:, start : start + size].reshape(-1)

    gain_one, shift_one, query_bias, value_bias, out_bias, gain_two, shift_two = (
        vector(QUART * index, QUART) for index in range(7)
    )
    up_bias = vector(7 * QUART, D)
    down_bias = vector(11 * QUART, QUART)

    segments = segment_ids[0]
    upstream = cotangent[0]

    hidden_in = own_tokens.astype(F32)
    normed_parts = [
        layer_norm(part.astype(F32), gain_one, shift_one).astype(BF) for part in tokens
    ]
    normed = normed_parts[0]
    normed_all = jnp.concatenate(normed_parts)
    queries = (
        jnp.dot(normed, full_qkv[:, :D], preferred_element_type=F32) + query_bias
    ).astype(BF)
    keys = jnp.dot(normed_all, full_qkv[:, D : 2 * D], preferred_element_type=F32).astype(BF)
    values = jnp.dot(normed_all, full_qkv[:, 2 * D :], preferred_element_type=F32)
    values = (values + value_bias).astype(BF)
    query_places = rank * rows + jnp.arange(rows)
    starts = [jnp.bitwise_xor(rank, flip) * rows for flip in range(4)]
    key_places = jnp.concatenate([start + jnp.arange(rows) for start in starts])
    key_segments = jnp.concatenate(
        [
            lax.dynamic_slice(segments, (start,), (rows,), allow_negative_indices=False)
            for start in starts
        ]
    )
    allowed = (key_segments[:rows, None] == key_segments[None, :]) & (
        query_places[:, None] >= key_places[None, :]
    )
    mask = jnp.where(allowed, 0.0, -1e30).astype(F32)
    mixed, log_total = attend_forward(queries, keys, values, mask)
    far_mlp = after(far_mlp, mixed)
    full_up, full_down = finish_mlp(w_up, w_down, got_rest, far_mlp, across_rest)
    middle = hidden_in + jnp.dot(mixed, full_out, preferred_element_type=F32) + out_bias
    normed_two = layer_norm(middle, gain_two, shift_two).astype(BF)
    upper = jnp.dot(normed_two, full_up, preferred_element_type=F32) + up_bias
    activated, slope = gelu_both(upper)
    activated = activated.astype(BF)
    block_output = middle + jnp.dot(activated, full_down, preferred_element_type=F32) + down_bias

    def paired(value):
        return value, swap_core(value)

    def paired_columns(value):
        width = value.shape[1] // 4
        blocks = [value[:, at * width : (at + 1) * width] for at in range(4)]
        even, odd = jnp.stack([blocks[0], blocks[2]]), jnp.stack([blocks[1], blocks[3]])
        mine = jnp.where(core == 0, even, odd)
        other = jnp.where(core == 0, odd, even)
        return mine, swap_core(other)

    upstream_wide = upstream.astype(F32)
    upstream_pair = paired(upstream)
    grad_down_bias = jnp.sum(upstream_wide, axis=0)
    activated_pair = paired_columns(activated)

    d_activated = jnp.dot(upstream, full_down.T, preferred_element_type=F32)
    d_upper = (d_activated * slope).astype(BF)
    grad_up_bias = jnp.sum(d_upper.astype(F32), axis=0)
    normed_two_pair, d_upper_pair = paired_columns(normed_two), paired(d_upper)
    no_vectors = jnp.zeros((2, 12, D), F32)
    grad_mlp = weight_grad(activated_pair, [upstream_pair], no_vectors, 2, 0, 0)
    grad_mlp = weight_grad(
        normed_two_pair, [d_upper_pair], no_vectors, 2, 0, 1, grad_mlp
    )
    mlp_part = lax.psum_scatter(
        grad_mlp.reshape(64 * PAD, D), ("y", "x"), scatter_dimension=0, tiled=True
    ).reshape(2, 2, PAD, D)

    d_normed_two = jnp.dot(d_upper, full_up.T, preferred_element_type=F32)
    norm_two_back = jax.vjp(layer_norm, middle, gain_two, shift_two)[1]
    d_middle_part, grad_gain_two, grad_shift_two = norm_two_back(d_normed_two)
    d_middle = upstream_wide + d_middle_part
    d_attended = d_middle.astype(BF)
    grad_out_bias = jnp.sum(d_attended.astype(F32), axis=0)
    mixed_pair, d_attended_pair = paired_columns(mixed), paired(d_attended)
    normed_pair = paired_columns(normed)

    d_mixed = jnp.dot(d_attended, full_out.T, preferred_element_type=F32).astype(BF)
    d_queries, d_both, d_beside = attend_backward(
        queries, keys, values, mask, log_total, after(d_mixed, grad_mlp)
    )
    d_beside = swap_core(d_beside)
    d_half = swap_half((d_both[1].astype(F32) + d_beside[1].astype(F32)).astype(BF))
    queries_pair = paired(d_queries)
    grad_attn = weight_grad(mixed_pair, [d_attended_pair], no_vectors, 1, 12, 0)
    d_half = after(after(after(d_half, grad_attn), queries_pair[1]), normed_pair[1])
    d_both = d_both[0].astype(F32) + d_beside[0].astype(F32) + d_half.astype(F32)
    d_both = d_both.astype(BF)
    d_keys, d_values = d_both[0], d_both[1]
    grad_query_bias = jnp.sum(d_queries.astype(F32), axis=0)
    grad_value_bias = jnp.sum(d_values.astype(F32), axis=0)
    rights = [queries_pair, paired(d_keys), paired(d_values)]
    d_normed = None
    for at, part in enumerate((d_queries, d_keys, d_values)):
        term = lax.dot_general(
            part,
            full_qkv[:, at * D : (at + 1) * D],
            (((1,), (1,)), ((), ())),
            preferred_element_type=F32,
        )
        d_normed = term if d_normed is None else d_normed + term
    norm_one_back = jax.vjp(layer_norm, hidden_in, gain_one, shift_one)[1]
    d_input_part, grad_gain_one, grad_shift_one = norm_one_back(d_normed)
    grad_input = d_middle + d_input_part

    vectors = jnp.concatenate(
        [
            value.reshape(4, -1)
            for value in (
                grad_gain_one,
                grad_shift_one,
                grad_query_bias,
                grad_value_bias,
                grad_out_bias,
                grad_gain_two,
                grad_shift_two,
                grad_down_bias,
                grad_up_bias,
            )
        ],
        axis=1,
    )
    even, odd = vectors[0::2], vectors[1::2]
    mine = jnp.where(core == 0, even, odd)
    other = jnp.where(core == 0, odd, even)
    mine = (mine + swap_core(other.astype(BF)).astype(F32)).astype(BF)
    mine = jnp.pad(mine.reshape(2, 12, VECTOR).astype(F32), ((0, 0), (0, 0), (0, D - VECTOR)))

    early = depth_sum(mlp_part.transpose(1, 0, 2, 3).reshape(2, 2 * PAD, D), zh, d_normed)
    grad_attn = weight_grad(normed_pair, rights, mine, 1, 0, 0, grad_attn)
    grad_attn = grad_attn.reshape(4, 4, 2, PAD, D)

    def cut(start, size):
        return lax.dynamic_slice(grad_attn, start, size, allow_negative_indices=False)

    def part_of(values):
        return lambda place: cut_row(values, place)

    def cut_row(values, place):
        return lax.dynamic_slice(
            values, (place, 0, 0), (1, PAD, D), allow_negative_indices=False
        )[0]

    one = ring_scatter_halves(
        lambda place: cut((0, place, 0, 0, 0), (4, 1, 1, PAD, D)).reshape(4, PAD, D), "x"
    )
    two = ring_scatter_halves(
        lambda place: cut((place, 0, 1, 0, 0), (1, 4, 1, PAD, D)).reshape(4, PAD, D), "y"
    )
    one, two = ring_scatter(part_of(one), "y"), ring_scatter(part_of(two), "x")
    attn_part = depth_sum(jnp.stack([one, two]), zh)
    parts = lax.all_gather(early, ("y", "x"), axis=0, tiled=True).reshape(16, 2, PAD, D)
    grad_down = unpack(parts[:, 0], D)
    grad_up = unpack(parts[:, 1], QUART)
    attn_part = after(attn_part, parts)
    one, two = ring_gather(attn_part[:40], "x"), ring_gather(attn_part[40:], "y")
    one, two = ring_gather(one, "y"), ring_gather(two, "x")
    two = after(after(two, grad_up), grad_down)
    grad_qkv, grad_out = unpack_pair(one, two)
    vectors = two[:, :3, SLICE - 40, :VECTOR].transpose(1, 0, 2).reshape(-1).astype(F32)

    def owned(start, size):
        return vectors[start : start + size]

    return (
        block_output[None],
        grad_input[None],
        owned(0, QUART),
        owned(QUART, QUART),
        grad_qkv,
        owned(2 * QUART, QUART),
        owned(3 * QUART, QUART),
        grad_out,
        owned(4 * QUART, QUART),
        owned(5 * QUART, QUART),
        owned(6 * QUART, QUART),
        grad_up,
        owned(8 * QUART, D),
        grad_down,
        owned(7 * QUART, QUART),
    )


def solution(mesh):
    grid = Mesh(mesh.devices.reshape(4, 4, 2, 2, 2), AXES)
    rep, grp = ("y", "x", "zl"), ("zh", "c")
    tokens = P(rep, grp, None)
    vector, matrix = P(grp), P(grp, None)
    params = (
        vector,
        vector,
        matrix,
        vector,
        vector,
        matrix,
        vector,
        vector,
        vector,
        matrix,
        vector,
        matrix,
        vector,
    )
    return jax.shard_map(
        body,
        mesh=grid,
        in_specs=(tokens, P(rep, None)) + params + (tokens,),
        out_specs=(tokens, tokens) + params,
        check_vma=False,
    )
```

```python
import functools

import jax
import jax.numpy as jnp
from jax import lax
from jax.experimental import pallas as pl
from jax.experimental.layout import Layout, with_layout_constraint
from jax.experimental.pallas import tpu as pltpu
from jax.sharding import Mesh
from jax.sharding import PartitionSpec as P

D = 1088
HEADS = 17
HEAD = 64
QUART = 272
SLICE = 68
PAD = 72
VECTOR = 272
AXES = ("y", "x", "zl", "zh", "c")
BF = jnp.bfloat16
F32 = jnp.float32


def layer_norm(values, gain, shift):
    centre = values - jnp.mean(values, axis=-1, keepdims=True)
    spread = jnp.mean(centre * centre, axis=-1, keepdims=True)
    return centre * lax.rsqrt(spread + 1e-05) * gain + shift


def gelu_both(values):
    below = 0.5 * (1.0 + lax.erf(values * 0.7071067811865476))
    density = jnp.exp(values * values * -0.5) * 0.3989422804014327
    return values * below, below + values * density


def rows_major(x):
    return with_layout_constraint(x, Layout(major_to_minor=tuple(range(x.ndim))))


def permute(x, axis, pairs):
    shape = x.shape
    if shape[-2] % 128 == 0 and shape[-1] % 128 != 0:
        x = x.reshape(-1, 64, shape[-1])
    return rows_major(lax.ppermute(rows_major(x), axis, pairs)).reshape(shape)


def rotate(x, axis, step):
    return permute(x, axis, [(at, (at + step) % 4) for at in range(4)])


def swap_core(x):
    return permute(x, "c", [(0, 1), (1, 0)])


def swap_half(x):
    return permute(x, "zh", [(0, 1), (1, 0)])


def swap_near(x):
    return permute(x, "zl", [(0, 1), (1, 0)])


def swap_far(x):
    return permute(x, ("zl", "zh"), [(0, 3), (3, 0), (1, 2), (2, 1)])


def swap_pair(x, axis):
    return permute(x, axis, [(0, 1), (1, 0), (2, 3), (3, 2)])


def after_kernel(x_ref, done_ref, out_ref):
    pass


def after(x, done):
    if done.size > 2**19:
        done = done.reshape((-1,) + done.shape[-2:])[0, :8, :128]
    return pl.pallas_call(
        after_kernel,
        out_shape=jax.ShapeDtypeStruct(x.shape, x.dtype),
        in_specs=[pl.BlockSpec(memory_space=pl.ANY)] * 2,
        out_specs=pl.BlockSpec(memory_space=pl.ANY),
        input_output_aliases={0: 0},
    )(x, done)


def rows_of(values, start, size):
    return lax.dynamic_slice(
        values, (start, 0), (size, values.shape[1]), allow_negative_indices=False
    )


def natural(parts, place):
    found = []
    for index in range(4):
        value = parts[index]
        for at in range(1, 4):
            value = jnp.where(place == at, parts[(index - at) % 4], value)
        found.append(value)
    return jnp.stack(found)


def ring_scatter(part, axis):
    place = lax.axis_index(axis)
    got = [rotate(part((place + step) & 3), axis, step) for step in (2, 1, 3)]
    total = part(place).astype(F32)
    for value in got:
        total = total + value.astype(F32)
    return total.astype(BF)


def ring_scatter_halves(part, axis):
    place = lax.axis_index(axis)
    far, ahead, behind = (part((place + step) & 3) for step in (2, 1, 3))
    half = far.shape[0] // 2
    from_behind, from_ahead = rotate(far[:half], axis, 1), rotate(far[half:], axis, -1)

    def added(value, more):
        return (value.astype(F32) + more.astype(F32)).astype(BF)

    ahead = jnp.concatenate([added(ahead[:half], from_behind), ahead[half:]])
    behind = jnp.concatenate([behind[:half], added(behind[half:], from_ahead)])
    one, two = rotate(ahead, axis, 1), rotate(behind, axis, -1)
    total = part(place).astype(F32) + one.astype(F32) + two.astype(F32)
    return total.astype(BF)


def ring_gather(piece, axis):
    far, behind, ahead = (rotate(piece, axis, step) for step in (2, 1, 3))
    return natural([piece, ahead, far, behind], lax.axis_index(axis))


def depth_sum(values, zh, done=None):
    mine = jnp.where(zh == 0, values[0], values[1])
    other = jnp.where(zh == 0, values[1], values[0])
    far, half, near = swap_far(other), swap_half(other), swap_near(mine)
    if done is not None:
        near = after(near, done)
    total = mine.astype(F32) + near.astype(F32) + far.astype(F32) + half.astype(F32)
    return total.astype(BF)


def assemble_kernel(spots, *refs):
    *parts, out, sems = refs
    rows = out.shape[0] // 4
    rank = lax.axis_index("zh") * 2 + lax.axis_index("c")
    quarter = lax.axis_index("y") % 2 * 2 + lax.axis_index("x") % 2
    copies = []
    for which, row, flip, start, turn, size in spots:
        at = jnp.bitwise_xor(rank, flip) * rows + start
        if turn is not None:
            at = at + jnp.bitwise_xor(quarter, turn) * size
        copy = pltpu.make_async_copy(
            parts[which].at[pl.ds(row, size)],
            out.at[pl.ds(pl.multiple_of(at, 16), size)],
            sems.at[len(copies)],
        )
        copy.start()
        copies.append(copy)
    for copy in copies:
        copy.wait()


def assemble(rows, parts, spots):
    columns = parts[0].shape[1]
    return pl.pallas_call(
        functools.partial(assemble_kernel, spots),
        out_shape=jax.ShapeDtypeStruct((rows * 4, columns), BF),
        in_specs=[pl.BlockSpec(memory_space=pltpu.VMEM)] * len(parts),
        out_specs=pl.BlockSpec(memory_space=pl.ANY),
        scratch_shapes=[pltpu.SemaphoreType.DMA((len(spots),))],
        compiler_params=pltpu.CompilerParams(vmem_limit_bytes=24 * 2**20),
        cost_estimate=pl.CostEstimate(
            flops=0, bytes_accessed=rows * columns * 16, transcendentals=0
        ),
    )(*parts)


def dot_nt(left, right):
    return lax.dot_general(left, right, (((1,), (1,)), ((), ())), preferred_element_type=F32)


def dot_tn(left, right):
    return lax.dot_general(left, right, (((0,), (0,)), ((), ())), preferred_element_type=F32)


def attend_forward_kernel(q_ref, k_ref, v_ref, mask_ref, mixed_ref, total_ref):
    mask = mask_ref[...]
    queries, keys, values = q_ref[...], k_ref[...], v_ref[...]
    mixed, totals = [], []
    for head in range(2):
        lanes = slice(head * HEAD, (head + 1) * HEAD)
        scores = dot_nt(queries[:, lanes], keys[:, lanes]) * 0.125 + mask
        highest = jnp.max(scores, axis=1, keepdims=True)
        powers = jnp.exp(scores - highest)
        total = jnp.sum(powers, axis=1, keepdims=True)
        probs = (powers * (1.0 / total)).astype(BF)
        value = jnp.dot(probs, values[:, lanes], preferred_element_type=F32)
        mixed.append(value)
        totals.append(jnp.broadcast_to(highest + jnp.log(total), value.shape))
    mixed_ref[...] = jnp.concatenate(mixed, axis=1).astype(BF)
    total_ref[...] = jnp.concatenate(totals, axis=1)


def attend_backward_kernel(
    q_ref, k_ref, v_ref, mask_ref, total_ref, d_mixed_ref, dq_ref, keep_ref, send_ref
):
    mask = mask_ref[...]
    queries, keys, values = q_ref[...], k_ref[...], v_ref[...]
    totals, d_mixed = total_ref[...], d_mixed_ref[...]
    d_query, d_key, d_value = [], [], []
    for head in range(2):
        lanes = slice(head * HEAD, (head + 1) * HEAD)
        query, key, upstream = queries[:, lanes], keys[:, lanes], d_mixed[:, lanes]
        scores = dot_nt(query, key) * 0.125 + mask
        probs = jnp.exp(scores - totals[:, lanes][:, :1])
        weighted = probs * dot_nt(upstream, values[:, lanes])
        centred = jnp.sum(weighted, axis=1, keepdims=True)
        d_scores = (weighted - probs * centred).astype(BF)
        d_query.append(jnp.dot(d_scores, key, preferred_element_type=F32) * 0.125)
        d_key.append(dot_tn(d_scores, query) * 0.125)
        d_value.append(dot_tn(probs.astype(BF), upstream))
    dq_ref[...] = jnp.concatenate(d_query, axis=1).astype(BF)
    rows = dq_ref.shape[0]
    for at, parts in enumerate((d_key, d_value)):
        whole = jnp.concatenate(parts, axis=1).astype(BF)
        keep_ref[0, at] = whole[:rows]
        send_ref[0, at] = whole[rows : 2 * rows]
        keep_ref[1, at] = whole[2 * rows : 3 * rows]
        send_ref[1, at] = whole[3 * rows :]


def pair_spec(rows):
    return pl.BlockSpec((rows, 2 * HEAD), lambda at: (0, at))


def attend_forward(queries, keys, values, mask):
    rows, length = mask.shape
    return pl.pallas_call(
        attend_forward_kernel,
        grid=((HEADS + 1) // 2,),
        out_shape=(
            jax.ShapeDtypeStruct((rows, D), BF),
            jax.ShapeDtypeStruct((rows, D), F32),
        ),
        in_specs=[
            pair_spec(rows),
            pair_spec(length),
            pair_spec(length),
            pl.BlockSpec(mask.shape, lambda at: (0, 0)),
        ],
        out_specs=(pair_spec(rows), pair_spec(rows)),
        compiler_params=pltpu.CompilerParams(vmem_limit_bytes=32 * 2**20),
        cost_estimate=pl.CostEstimate(
            flops=4 * rows * length * D,
            bytes_accessed=24 * rows * D,
            transcendentals=HEADS * rows * length,
        ),
    )(queries, keys, values, mask)


def attend_backward(queries, keys, values, mask, totals, d_mixed):
    rows, length = mask.shape
    both = jax.ShapeDtypeStruct((2, 2, rows, D), BF)
    both_spec = pl.BlockSpec((2, 2, rows, 2 * HEAD), lambda at: (0, 0, 0, at))
    return pl.pallas_call(
        attend_backward_kernel,
        grid=((HEADS + 1) // 2,),
        out_shape=(jax.ShapeDtypeStruct((rows, D), BF), both, both),
        in_specs=[
            pair_spec(rows),
            pair_spec(length),
            pair_spec(length),
            pl.BlockSpec(mask.shape, lambda at: (0, 0)),
            pair_spec(rows),
            pair_spec(rows),
        ],
        out_specs=(pair_spec(rows), both_spec, both_spec),
        compiler_params=pltpu.CompilerParams(vmem_limit_bytes=32 * 2**20),
        cost_estimate=pl.CostEstimate(
            flops=10 * rows * length * D,
            bytes_accessed=48 * rows * D,
            transcendentals=HEADS * rows * length,
        ),
    )(queries, keys, values, mask, totals, d_mixed)


def weight_grad_kernel(count, first, *refs):
    lefts, rights = refs[:2], refs[2 : 2 + 2 * count]
    vector_ref, out_ref = refs[2 + 2 * count], refs[-1]
    left, left_other = lefts[0][0], lefts[1][0]
    pieces = left.shape[1] // SLICE
    done = 0
    for own, other in zip(rights[::2], rights[1::2]):
        for at in range(own.shape[-1] // D):
            lanes = slice(at * D, (at + 1) * D)
            product = dot_tn(left, own[:, lanes]) + dot_tn(left_other, other[:, lanes])
            for piece in range(pieces):
                part = product[piece * SLICE : (piece + 1) * SLICE]
                empty = jnp.zeros((PAD - SLICE, D), F32)
                if first == 0 and count == 3:
                    row = vector_ref[0, done : done + 1]
                    empty = jnp.concatenate([row, empty[1:]])
                out_ref[done, 0, 0] = jnp.concatenate([part, empty]).astype(BF)
                done += 1


def weight_grad(lefts, rights, vectors, slots, first, slot, buffer=None):
    _, tokens, width = lefts[0].shape
    rights = [value for pair in rights for value in pair]
    blocks = sum(value.shape[1] for value in rights[::2]) // D
    pieces = blocks * (width // SLICE)
    in_specs = [pl.BlockSpec((1, tokens, width), lambda at: (at, 0, 0))] * 2
    in_specs += [pl.BlockSpec(value.shape, lambda at: (0, 0)) for value in rights]
    in_specs += [pl.BlockSpec((1,) + vectors.shape[1:], lambda at: (at, 0, 0))]
    more = () if buffer is None else (buffer,)
    operands = (*lefts, *rights, vectors)
    return pl.pallas_call(
        functools.partial(weight_grad_kernel, len(rights) // 2, first),
        grid=(2,),
        out_shape=jax.ShapeDtypeStruct((16, slots, 2, PAD, D), BF),
        in_specs=in_specs + [pl.BlockSpec(memory_space=pl.ANY)] * len(more),
        out_specs=pl.BlockSpec(
            (pieces, 1, 1, PAD, D), lambda at: (first // pieces, slot, at, 0, 0)
        ),
        input_output_aliases={len(operands): 0} if more else {},
        compiler_params=pltpu.CompilerParams(vmem_limit_bytes=48 * 2**20),
        cost_estimate=pl.CostEstimate(
            flops=8 * tokens * width * blocks * D,
            bytes_accessed=2 * sum(value.size for value in operands) + 4 * pieces * PAD * D,
            transcendentals=0,
        ),
    )(*operands, *more)


def unpack_kernel(in_ref, out_ref):
    count, across = out_ref.shape[0] // SLICE, out_ref.shape[1] // D
    for at in range(across):
        for piece in range(count):
            part = in_ref[at * count + piece].astype(F32)[:SLICE]
            out_ref[piece * SLICE : (piece + 1) * SLICE, at * D : (at + 1) * D] = part


def unpack(pieces, rows):
    columns = pieces.shape[0] * SLICE // rows * D
    return pl.pallas_call(
        unpack_kernel,
        out_shape=jax.ShapeDtypeStruct((rows, columns), F32),
        in_specs=[pl.BlockSpec(memory_space=pltpu.VMEM)],
        out_specs=pl.BlockSpec(memory_space=pltpu.VMEM),
        compiler_params=pltpu.CompilerParams(vmem_limit_bytes=24 * 2**20),
        cost_estimate=pl.CostEstimate(
            flops=0, bytes_accessed=pieces.size * 6, transcendentals=0
        ),
    )(pieces)


def unpack_pair_kernel(one_ref, two_ref, wide_ref, last_ref):
    for down in range(4):
        for across in range(4):
            one, two = one_ref[down, across].astype(F32), two_ref[across, down].astype(F32)
            part = jnp.concatenate([one, two[: SLICE - one.shape[0]]])
            lines = slice(across * SLICE, (across + 1) * SLICE)
            if down < 3:
                wide_ref[lines, down * D : (down + 1) * D] = part
            else:
                last_ref[lines, :] = part


def unpack_pair(one, two):
    return pl.pallas_call(
        unpack_pair_kernel,
        out_shape=(
            jax.ShapeDtypeStruct((QUART, 3 * D), F32),
            jax.ShapeDtypeStruct((QUART, D), F32),
        ),
        in_specs=[pl.BlockSpec(memory_space=pltpu.VMEM)] * 2,
        out_specs=(pl.BlockSpec(memory_space=pltpu.VMEM),) * 2,
        compiler_params=pltpu.CompilerParams(vmem_limit_bytes=24 * 2**20),
        cost_estimate=pl.CostEstimate(
            flops=0, bytes_accessed=(one.size + two.size) * 6, transcendentals=0
        ),
    )(one, two)


def gather_quarters(shard):
    across, down = lax.axis_index("x") & 1, lax.axis_index("y") & 1
    piece = rows_of(shard, (down * 2 + across) * 64, 64)
    got = swap_far(jnp.concatenate([piece, shard[256:]]))
    mine = got[:64]
    by_x, by_y = swap_pair(mine, "x"), swap_pair(mine, "y")
    last = swap_pair(by_y, "x")
    return got, jnp.concatenate([got, by_x, by_y, last])


def widened(value):
    size = value.shape[0] // 4
    return jnp.concatenate([value[at * size : (at + 1) * size] for at in range(4)], axis=1)


def narrowed(value):
    return jnp.stack([value[:, :, at * D : (at + 1) * D] for at in range(4)], axis=1).reshape(-1, D)


def start_mlp(w_up, w_down, spot, done, done_rest):
    sent = [rows_of(w_up, spot * 16, 16), widened(rows_of(w_down, spot * 64, 64))]
    got = swap_far(after(jnp.concatenate(sent), done))
    far = lax.all_gather(got, ("y", "x"), axis=0, tiled=True)
    rest = swap_far(after(jnp.concatenate([w_up[256:], widened(w_down[1024:])]), done_rest))
    return far, rest, swap_core(rest)


def finish_mlp(w_up, w_down, rest, far, across_rest):
    across = swap_core(far).reshape(16, 32, 4 * D)
    far = far.reshape(16, 32, 4 * D)
    up = assemble(
        QUART,
        (
            w_up,
            swap_core(w_up),
            far[:, :16].reshape(256, 4 * D),
            rest,
            across[:, :16].reshape(256, 4 * D),
            across_rest,
        ),
        (
            (0, 0, 0, 0, None, QUART),
            (1, 0, 1, 0, None, QUART),
            (2, 0, 2, 0, None, 256),
            (3, 0, 2, 256, None, 16),
            (4, 0, 3, 0, None, 256),
            (5, 0, 3, 256, None, 16),
        ),
    )
    down = assemble(
        D,
        (
            w_down,
            swap_core(w_down),
            narrowed(far[:, 16:]),
            narrowed(rest[None, 16:32]),
            narrowed(across[:, 16:]),
            narrowed(across_rest[None, 16:32]),
        ),
        (
            (0, 0, 0, 0, None, D),
            (1, 0, 1, 0, None, D),
            (2, 0, 2, 0, None, 1024),
            (3, 0, 2, 1024, None, 64),
            (4, 0, 3, 0, None, 1024),
            (5, 0, 3, 1024, None, 64),
        ),
    )
    return up, down


def body(
    block_input,
    segment_ids,
    attn_gain,
    attn_shift,
    w_qkv,
    bias_query,
    bias_value,
    w_out,
    bias_out,
    mlp_gain,
    mlp_shift,
    w_up,
    bias_up,
    w_down,
    bias_down,
    cotangent,
):
    core, zh = lax.axis_index("c"), lax.axis_index("zh")
    rank = zh * 2 + core
    spot = lax.axis_index("y") * 4 + lax.axis_index("x")
    small = jnp.concatenate(
        [
            attn_gain,
            attn_shift,
            bias_query,
            bias_value,
            bias_out,
            mlp_gain,
            mlp_shift,
            bias_up,
            bias_down,
        ]
    )
    small = jnp.pad(small.reshape(3, D), ((0, 13), (0, 0)))
    rows = block_input.shape[1]
    own_tokens = block_input[0]
    got_qkv, far_parts = gather_quarters(w_qkv)
    with_small = jnp.concatenate([own_tokens, small])
    half = swap_half(after(with_small, got_qkv))
    token_parts = [with_small, swap_core(with_small), half, swap_core(half)]
    tokens = [part[:rows] for part in token_parts]
    smalls = [part[rows : rows + 3].reshape(-1).astype(F32) for part in token_parts]
    across_parts = swap_core(far_parts)
    far_mlp, got_rest, across_rest = start_mlp(
        w_up, w_down, spot, far_parts, across_parts
    )
    turns = ((0, 0, 0, 64), (80, 0, 1, 64), (144, 0, 2, 64), (208, 0, 3, 64), (64, 256, None, 16))
    full_qkv = assemble(
        QUART,
        (w_qkv, swap_core(w_qkv), far_parts, across_parts),
        ((0, 0, 0, 0, None, QUART), (1, 0, 1, 0, None, QUART))
        + tuple((2, row, 2, *turn) for row, *turn in turns)
        + tuple((3, row, 3, *turn) for row, *turn in turns),
    )
    far_out = after(swap_far(after(w_out, half)), full_qkv)
    full_out = assemble(
        QUART,
        (w_out, swap_core(w_out), far_out, swap_core(far_out)),
        tuple((flip, 0, flip, 0, None, QUART) for flip in range(4)),
    )

    ordered = []
    for index in range(4):
        value = smalls[index]
        for at in range(1, 4):
            value = jnp.where(rank == at, smalls[index ^ at], value)
        ordered.append(value)
    ordered = jnp.stack(ordered)

    def vector(start, size):
        return ordered[:, start : start + size].reshape(-1)

    gain_one, shift_one, query_bias, value_bias, out_bias, gain_two, shift_two = (
        vector(QUART * index, QUART) for index in range(7)
    )
    up_bias = vector(7 * QUART, D)
    down_bias = vector(11 * QUART, QUART)

    segments = segment_ids[0]
    upstream = cotangent[0]

    hidden_in = own_tokens.astype(F32)
    normed_parts = [
        layer_norm(part.astype(F32), gain_one, shift_one).astype(BF) for part in tokens
    ]
    normed = normed_parts[0]
    normed_all = jnp.concatenate(normed_parts)
    queries = (
        jnp.dot(normed, full_qkv[:, :D], preferred_element_type=F32) + query_bias
    ).astype(BF)
    keys = jnp.dot(normed_all, full_qkv[:, D : 2 * D], preferred_element_type=F32).astype(BF)
    values = jnp.dot(normed_all, full_qkv[:, 2 * D :], preferred_element_type=F32)
    values = (values + value_bias).astype(BF)
    query_places = rank * rows + jnp.arange(rows)
    starts = [jnp.bitwise_xor(rank, flip) * rows for flip in range(4)]
    key_places = jnp.concatenate([start + jnp.arange(rows) for start in starts])
    key_segments = jnp.concatenate(
        [
            lax.dynamic_slice(segments, (start,), (rows,), allow_negative_indices=False)
            for start in starts
        ]
    )
    allowed = (key_segments[:rows, None] == key_segments[None, :]) & (
        query_places[:, None] >= key_places[None, :]
    )
    mask = jnp.where(allowed, 0.0, -1e30).astype(F32)
    mixed, log_total = attend_forward(queries, keys, values, mask)
    far_mlp = after(far_mlp, mixed)
    full_up, full_down = finish_mlp(w_up, w_down, got_rest, far_mlp, across_rest)
    middle = hidden_in + jnp.dot(mixed, full_out, preferred_element_type=F32) + out_bias
    normed_two = layer_norm(middle, gain_two, shift_two).astype(BF)
    upper = jnp.dot(normed_two, full_up, preferred_element_type=F32) + up_bias
    activated, slope = gelu_both(upper)
    activated = activated.astype(BF)
    block_output = middle + jnp.dot(activated, full_down, preferred_element_type=F32) + down_bias

    def paired(value):
        return value, swap_core(value)

    def paired_columns(value):
        width = value.shape[1] // 4
        blocks = [value[:, at * width : (at + 1) * width] for at in range(4)]
        even, odd = jnp.stack([blocks[0], blocks[2]]), jnp.stack([blocks[1], blocks[3]])
        mine = jnp.where(core == 0, even, odd)
        other = jnp.where(core == 0, odd, even)
        return mine, swap_core(other)

    upstream_wide = upstream.astype(F32)
    upstream_pair = paired(upstream)
    grad_down_bias = jnp.sum(upstream_wide, axis=0)
    activated_pair = paired_columns(activated)

    d_activated = jnp.dot(upstream, full_down.T, preferred_element_type=F32)
    d_upper = (d_activated * slope).astype(BF)
    grad_up_bias = jnp.sum(d_upper.astype(F32), axis=0)
    normed_two_pair, d_upper_pair = paired_columns(normed_two), paired(d_upper)
    no_vectors = jnp.zeros((2, 12, D), F32)
    grad_mlp = weight_grad(activated_pair, [upstream_pair], no_vectors, 2, 0, 0)
    grad_mlp = weight_grad(
        normed_two_pair, [d_upper_pair], no_vectors, 2, 0, 1, grad_mlp
    )
    mlp_part = lax.psum_scatter(
        grad_mlp.reshape(64 * PAD, D), ("y", "x"), scatter_dimension=0, tiled=True
    ).reshape(2, 2, PAD, D)

    d_normed_two = jnp.dot(d_upper, full_up.T, preferred_element_type=F32)
    norm_two_back = jax.vjp(layer_norm, middle, gain_two, shift_two)[1]
    d_middle_part, grad_gain_two, grad_shift_two = norm_two_back(d_normed_two)
    d_middle = upstream_wide + d_middle_part
    d_attended = d_middle.astype(BF)
    grad_out_bias = jnp.sum(d_attended.astype(F32), axis=0)
    mixed_pair, d_attended_pair = paired_columns(mixed), paired(d_attended)
    normed_pair = paired_columns(normed)

    d_mixed = jnp.dot(d_attended, full_out.T, preferred_element_type=F32).astype(BF)
    d_queries, d_both, d_beside = attend_backward(
        queries, keys, values, mask, log_total, after(d_mixed, grad_mlp)
    )
    d_beside = swap_core(d_beside)
    d_half = swap_half((d_both[1].astype(F32) + d_beside[1].astype(F32)).astype(BF))
    queries_pair = paired(d_queries)
    grad_attn = weight_grad(mixed_pair, [d_attended_pair], no_vectors, 1, 12, 0)
    d_half = after(after(after(d_half, grad_attn), queries_pair[1]), normed_pair[1])
    d_both = d_both[0].astype(F32) + d_beside[0].astype(F32) + d_half.astype(F32)
    d_both = d_both.astype(BF)
    d_keys, d_values = d_both[0], d_both[1]
    grad_query_bias = jnp.sum(d_queries.astype(F32), axis=0)
    grad_value_bias = jnp.sum(d_values.astype(F32), axis=0)
    rights = [queries_pair, paired(d_keys), paired(d_values)]
    d_normed = None
    for at, part in enumerate((d_queries, d_keys, d_values)):
        term = lax.dot_general(
            part,
            full_qkv[:, at * D : (at + 1) * D],
            (((1,), (1,)), ((), ())),
            preferred_element_type=F32,
        )
        d_normed = term if d_normed is None else d_normed + term
    norm_one_back = jax.vjp(layer_norm, hidden_in, gain_one, shift_one)[1]
    d_input_part, grad_gain_one, grad_shift_one = norm_one_back(d_normed)
    grad_input = d_middle + d_input_part

    vectors = jnp.concatenate(
        [
            value.reshape(4, -1)
            for value in (
                grad_gain_one,
                grad_shift_one,
                grad_query_bias,
                grad_value_bias,
                grad_out_bias,
                grad_gain_two,
                grad_shift_two,
                grad_down_bias,
                grad_up_bias,
            )
        ],
        axis=1,
    )
    even, odd = vectors[0::2], vectors[1::2]
    mine = jnp.where(core == 0, even, odd)
    other = jnp.where(core == 0, odd, even)
    mine = (mine + swap_core(other.astype(BF)).astype(F32)).astype(BF)
    mine = jnp.pad(mine.reshape(2, 12, VECTOR).astype(F32), ((0, 0), (0, 0), (0, D - VECTOR)))

    grad_attn = weight_grad(normed_pair, rights, mine, 1, 0, 0, grad_attn)
    grad_attn = grad_attn.reshape(4, 4, 2, PAD, D)

    def cut(start, size):
        return lax.dynamic_slice(grad_attn, start, size, allow_negative_indices=False)

    def part_of(values):
        return lambda place: cut_row(values, place)

    def cut_row(values, place):
        return lax.dynamic_slice(
            values, (place, 0, 0), (1, PAD, D), allow_negative_indices=False
        )[0]

    one = ring_scatter_halves(
        lambda place: cut((0, place, 0, 0, 0), (4, 1, 1, PAD, D)).reshape(4, PAD, D), "x"
    )
    two = ring_scatter_halves(
        lambda place: cut((place, 0, 1, 0, 0), (1, 4, 1, PAD, D)).reshape(4, PAD, D), "y"
    )
    mlp_part = after(mlp_part, one)
    early = depth_sum(mlp_part.transpose(1, 0, 2, 3).reshape(2, 2 * PAD, D), zh)
    one, two = ring_scatter(part_of(one), "y"), ring_scatter(part_of(two), "x")
    attn_part = depth_sum(jnp.stack([one, two]), zh)
    parts = lax.all_gather(early, ("y", "x"), axis=0, tiled=True).reshape(16, 2, PAD, D)
    grad_down = unpack(parts[:, 0], D)
    grad_up = unpack(parts[:, 1], QUART)
    one, two = ring_gather(attn_part[:40], "x"), ring_gather(attn_part[40:], "y")
    one, two = ring_gather(one, "y"), ring_gather(two, "x")
    grad_qkv, grad_out = unpack_pair(one, two)
    vectors = two[:, :3, SLICE - 40, :VECTOR].transpose(1, 0, 2).reshape(-1).astype(F32)

    def owned(start, size):
        return vectors[start : start + size]

    return (
        block_output[None],
        grad_input[None],
        owned(0, QUART),
        owned(QUART, QUART),
        grad_qkv,
        owned(2 * QUART, QUART),
        owned(3 * QUART, QUART),
        grad_out,
        owned(4 * QUART, QUART),
        owned(5 * QUART, QUART),
        owned(6 * QUART, QUART),
        grad_up,
        owned(8 * QUART, D),
        grad_down,
        owned(7 * QUART, QUART),
    )


def solution(mesh):
    grid = Mesh(mesh.devices.reshape(4, 4, 2, 2, 2), AXES)
    rep, grp = ("y", "x", "zl"), ("zh", "c")
    tokens = P(rep, grp, None)
    vector, matrix = P(grp), P(grp, None)
    params = (
        vector,
        vector,
        matrix,
        vector,
        vector,
        matrix,
        vector,
        vector,
        vector,
        matrix,
        vector,
        matrix,
        vector,
    )
    return jax.shard_map(
        body,
        mesh=grid,
        in_specs=(tokens, P(rep, None)) + params + (tokens,),
        out_specs=(tokens, tokens) + params,
        check_vma=False,
    )
```
